32 devices in a mesh: groups: 2 (over y), seq: 16 (over z, x, core), mp: 1.
Axes of the slice: x: 2, y: 2, z: 4, core: 2. Of those that a mesh axis runs over, the one named last changes fastest.
Arguments:
- hidden: bfloat16 [7200, 5120], P(('groups', 'seq'), 'mp'), parts along dimension 0, may hold values from -6 to 6
- modulation: float32 [4, 5120], P('groups', 'mp'), parts along dimension 0, may hold values from -3 to 3
- head_weight: bfloat16 [5120, 64], P('mp'), may hold values from -0.078125 to 0.078125
- head_bias: float32 [64], P('mp'), may hold values from -3 to 3
- residual: float32 [64, 7200], P('mp', ('groups', 'seq')), parts along dimension 1, may hold values from -4 to 4
- latent: float32 [64, 7200], P('mp', ('groups', 'seq')), parts along dimension 1, may hold values from -6 to 6
- band_gain: float32 [2, 16], P(None, 'mp'), may hold values from 0.5 to 2
- cut_rows: int32 [2], P('groups'), parts along dimension 0, may hold values from 0 to 45
- cut_cols: int32 [2], P('groups'), parts along dimension 0, may hold values from 0 to 80
- skip_flags: int32 [100], P('groups'), parts along dimension 0, may hold values 0 or 1
- step_index: int32 [2], P('groups'), parts along dimension 0, may hold values from 0 to 49
Outputs:
- velocity: float32 [64, 7200], P('mp', ('groups', 'seq')), parts along dimension 1
- latent_next: float32 [64, 7200], P('mp', ('groups', 'seq')), parts along dimension 1
The draws below stay inside these ranges and needn't reach their ends.
There are 2 independent parts, one for each index of `groups`. The reference program is written for one: setup_inputs(seed, part) draws one part's arguments, and reference() takes and returns one part's arrays. A program takes and returns all parts, laid end to end along the dimension named above; an argument that names none is the same for every part. Nothing has to cross between parts.
Inputs may be any that keep to these rules, and one draw needn't show every extreme that they name: cut_rows[f] and cut_cols[f] belong to frame f.
All inputs are finite; a program needn't handle non-finite values.
Results may differ from the reference program's by a relative error of at most 0.0019.
Values sent between devices are 32-bit elements; how exact they have to be, the bound alone decides.
A program may use at most 64 MiB of HBM per device.

```python
import math
import jax
import jax.numpy as jnp
from jax import lax

D = 5120
OUTC = 16
PCH = 64
H = 90
W = 160
PH = 45
PW = 80
NSTEP = 50
TOKENS = 3600
FRAMES = 1


def plant(drawn, own_key, smallest, top_value):
    place = [jax.random.randint(jax.random.fold_in(own_key, axis), (), 0, length) for axis, length in enumerate(drawn.shape)]
    main_axis = drawn.shape.index(max(drawn.shape))
    neighbour = place[:main_axis] + [(place[main_axis] + 1) % drawn.shape[main_axis]] + place[main_axis + 1:]
    return drawn.at[tuple(place)].set(smallest).at[tuple(neighbour)].set(top_value)


def shard_levels(stream_key, dims, shards, least, top_value):
    level = 1.0
    for dim, shards_of in shards:
        heights = jax.random.uniform(jax.random.fold_in(jax.random.fold_in(stream_key, 6), dim), (shards_of,), jnp.float32, least / len(shards), top_value / len(shards))
        level = level * jnp.repeat(jnp.exp(heights), dims[dim] // shards_of).reshape((-1,) + (1,) * (len(dims) - 1 - dim))
    return level


def centred(stream_key, extent, width, limit, pieces=(), kind=jnp.bfloat16):
    values = jax.random.normal(stream_key, extent, jnp.float32) * width
    if len(pieces) > 0:
        values = shard_levels(stream_key, extent, pieces, -0.22, 0.18) * values
    return jnp.clip(values, min=-limit, max=limit).astype(kind)


def setup_inputs(seed: int = 0, part: int = 0) -> dict:
    seeds = jax.random.split(jax.random.key(seed), 12)
    part_splits = jax.random.split(jax.random.fold_in(seeds[11], part), 12)
    return {
        "hidden": centred(part_splits[0], (TOKENS, D), 1.0, 6.0, ((0, 16),)),
        "modulation": centred(part_splits[1], (2, D), 0.5, 3.0, (), jnp.float32),
        "head_weight": centred(seeds[2], (D, PCH), D ** -0.5, 0.078125),
        "head_bias": centred(seeds[3], (PCH,), 0.5, 3.0, (), jnp.float32),
        "residual": centred(part_splits[4], (PCH, TOKENS), 0.3, 4.0, ((1, 16),), jnp.float32),
        "latent": centred(part_splits[5], (PCH, TOKENS), 1.0, 6.0, ((1, 16),), jnp.float32),
        "band_gain": jnp.clip(jnp.exp(jax.random.uniform(seeds[6], (2, OUTC), jnp.float32, math.log(0.5), math.log(2.0))), 0.5, 2.0),
        "cut_rows": jax.random.randint(part_splits[7], (FRAMES,), 0, PH + 1).astype(jnp.int32),
        "cut_cols": jax.random.randint(part_splits[8], (FRAMES,), 0, PW + 1).astype(jnp.int32),
        "skip_flags": plant((jax.random.randint(part_splits[9], (NSTEP,), 0, 2) < 1).astype(jnp.int32), jax.random.fold_in(part_splits[9], 1), 0, 1),
        "step_index": jax.random.randint(part_splits[10], (1,), 0, NSTEP).astype(jnp.int32),
    }


EPSILON = 1e-06
GUIDE_EXTRA = 4.0
SHIFT_FACTOR = 5.0

def sigma_at(step_number):
    remain = 1.0 - step_number.astype(jnp.float32) / NSTEP
    return SHIFT_FACTOR * remain / (1.0 + (SHIFT_FACTOR - 1.0) * remain)

def band_weights(skip_flags, step_index, band_gain):
    current = step_index[0]
    counter = jnp.arange(NSTEP, dtype=jnp.int32)
    computed = (skip_flags == 0) & (counter <= current)
    last_full = jnp.max(jnp.where(computed, counter, -1))
    spacing = (current - last_full).astype(jnp.float32)
    gap_ratio = spacing / (spacing + 2.0)
    return (band_gain[0] * (1.0 + gap_ratio), band_gain[1] * (1.0 - 0.5 * gap_ratio))

def reference(hidden, modulation, head_weight, head_bias, residual, latent, band_gain, cut_rows, cut_cols, skip_flags, step_index):
    frame_tokens = PH * PW

    def head_frame(frame_block):
        values = frame_block.astype(jnp.float32)
        average = lax.optimization_barrier(jnp.sum(values, axis=1)) / D
        second = lax.optimization_barrier(jnp.sum(values * values, axis=1)) / D
        scale_inv = lax.rsqrt(second - average * average + EPSILON)
        normed = ((values - average[:, None]) * scale_inv[:, None] * (1.0 + modulation[1]) + modulation[0]).astype(jnp.bfloat16)
        return jnp.dot(normed, head_weight, preferred_element_type=jnp.float32)
    head_frames = lax.map(head_frame, hidden.reshape(FRAMES, frame_tokens, D))
    conditional = head_frames.reshape(TOKENS, PCH).T + head_bias[:, None]
    planes = residual.reshape(OUTC, 2, 2, FRAMES, PH, PW).transpose(3, 0, 4, 1, 5, 2).reshape(FRAMES, OUTC, H, W)
    row_range = jnp.arange(H, dtype=jnp.int32)
    col_range = jnp.arange(W, dtype=jnp.int32)
    rows_freq = jnp.minimum(row_range, H - row_range)
    cols_freq = jnp.minimum(col_range, W - col_range)
    keep_rows = rows_freq[None, :] <= cut_rows[:, None]
    keep_cols = cols_freq[None, :] <= cut_cols[:, None]
    kept_modes = (keep_rows[:, :, None] & keep_cols[:, None, :]).astype(jnp.float32)
    spectrum = jnp.fft.fft2(planes)
    low_planes = jnp.real(jnp.fft.ifft2(spectrum * kept_modes[:, None, :, :])).astype(jnp.float32)
    low_band = low_planes.reshape(FRAMES, OUTC, PH, 2, PW, 2).transpose(1, 3, 5, 0, 2, 4).reshape(PCH, TOKENS)
    high_band = residual - low_band
    w_low, w_high = band_weights(skip_flags, step_index, band_gain)
    row_low = jnp.repeat(w_low, 4)[:, None]
    row_high = jnp.repeat(w_high, 4)[:, None]
    velocity = conditional + GUIDE_EXTRA * (row_low * low_band + row_high * high_band)
    current = step_index[0]
    latent_next = latent + (sigma_at(current + 1) - sigma_at(current)) * velocity
    return (velocity, latent_next)
```

```python
import functools
import math

import jax
import jax.numpy as jnp
import ml_dtypes
import numpy as np
from jax import lax
from jax.experimental import pallas as pl
from jax.experimental.pallas import tpu as pltpu
from jax.sharding import PartitionSpec as P

D = 5120
H = 90
W = 160
PH = 45
PW = 80
NSTEP = 50


EPSILON = 1e-06
GUIDE_EXTRA = 4.0
SHIFT_FACTOR = 5.0
HIGHEST = lax.Precision.HIGHEST


def from_partner(value, axis, bit):
    mask = 2**bit
    pairs = [(source, source ^ mask) for source in range(lax.axis_size(axis))]
    return lax.ppermute(value, axis, pairs)


def sigma_at(step_number):
    remain = 1.0 - step_number.astype(jnp.float32) / NSTEP
    return SHIFT_FACTOR * remain / (1.0 + (SHIFT_FACTOR - 1.0) * remain)


def band_weights(skip_flags, step_index, band_gain):
    current = step_index[0]
    counter = jnp.arange(NSTEP, dtype=jnp.int32)
    computed = (skip_flags == 0) & (counter <= current)
    last_full = jnp.max(jnp.where(computed, counter, -1))
    spacing = (current - last_full).astype(jnp.float32)
    gap_ratio = spacing / (spacing + 2.0)
    return (band_gain[0] * (1.0 + gap_ratio), band_gain[1] * (1.0 - 0.5 * gap_ratio))


def band_matrix(length, cutoff):
    counter = jnp.arange(length, dtype=jnp.int32)
    product = counter[:, None] * counter[None, :] % length
    angles = 2.0 * math.pi / length * product.astype(jnp.float32)
    cosine = jnp.cos(angles)
    sine_table = jnp.sin(angles)
    kept_modes = (jnp.minimum(counter, length - counter) <= cutoff).astype(jnp.float32)
    summed = jnp.dot(cosine * kept_modes, cosine.T, precision=HIGHEST) + jnp.dot(
        sine_table * kept_modes, sine_table.T, precision=HIGHEST
    )
    return summed / length


def gathered_body(
    hidden,
    modulation,
    head_weight,
    head_bias,
    residual,
    latent,
    band_gain,
    cut_rows,
    cut_cols,
    skip_flags,
    step_index,
):
    values = hidden.astype(jnp.float32)
    moments = lax.psum((jnp.sum(values, axis=1), jnp.sum(values * values, axis=1)), "mp")
    average = moments[0] / D
    scale_inv = lax.rsqrt(moments[1] / D - average * average + EPSILON)
    normed = (
        (values - average[:, None]) * scale_inv[:, None] * (1.0 + modulation[1]) + modulation[0]
    ).astype(jnp.bfloat16)
    conditional = (
        lax.psum_scatter(
            lax.dot_general(
                head_weight, normed, (((0,), (1,)), ((), ())), preferred_element_type=jnp.float32
            ),
            "mp",
            scatter_dimension=0,
            tiled=True,
        )
        + head_bias[:, None]
    )
    local_rows = residual.shape[0]
    local_tokens = residual.shape[1]
    frame_tokens = PH * PW
    members = frame_tokens // local_tokens
    seq_index = lax.axis_index("seq")
    position = seq_index % members
    frame_index = seq_index // members
    frame_data = residual
    for section_bit in range(members.bit_length() - 1):
        partner = from_partner(frame_data, "seq", section_bit)
        upper_half = seq_index // (1 << section_bit) % 2 == 1
        frame_data = jnp.where(
            upper_half,
            jnp.concatenate([partner, frame_data], axis=1),
            jnp.concatenate([frame_data, partner], axis=1),
        )
    channels = local_rows // 4
    planes = (
        frame_data.reshape(channels, 2, 2, PH, PW).transpose(0, 3, 1, 4, 2).reshape(channels, H, W)
    )
    row_filter = band_matrix(H, cut_rows[frame_index])
    col_filter = band_matrix(W, cut_cols[frame_index])
    row_total = min(local_tokens // PW + 2, PH)
    first_row = jnp.minimum(position * local_tokens // PW, PH - row_total)
    row_part = lax.dynamic_slice_in_dim(row_filter, 2 * first_row, 2 * row_total, 0)
    partial_rows = jnp.einsum("ij,cjw->ciw", row_part, planes, precision=HIGHEST)
    low_rows = jnp.dot(
        partial_rows.reshape(channels * 2 * row_total, W), col_filter, precision=HIGHEST
    ).reshape(channels, 2 * row_total, W)
    low_tokens = (
        low_rows.reshape(channels, row_total, 2, PW, 2)
        .transpose(0, 2, 4, 1, 3)
        .reshape(local_rows, row_total * PW)
    )
    low_band = lax.dynamic_slice_in_dim(
        low_tokens, position * local_tokens - first_row * PW, local_tokens, 1
    )
    high_band = residual - low_band
    w_low, w_high = band_weights(skip_flags, step_index, band_gain)
    row_low = jnp.repeat(w_low, 4)[:, None]
    row_high = jnp.repeat(w_high, 4)[:, None]
    velocity = conditional + GUIDE_EXTRA * (row_low * low_band + row_high * high_band)
    current = step_index[0]
    latent_next = latent + (sigma_at(current + 1) - sigma_at(current)) * velocity
    return (velocity, latent_next)


LANES = 128
CHUNK = 512
MESH = pl.DeviceIdType.MESH


def real_basis(length):
    place = np.arange(length)[:, None]
    column = np.arange(length)[None, :]
    frequency = (column + 1) // 2
    angle = 2.0 * np.pi * (place * frequency % length) / length
    basis = np.where(column % 2 == 1, np.cos(angle), np.sin(angle)) * math.sqrt(2.0 / length)
    basis[:, 0] = 1.0 / math.sqrt(length)
    if length % 2 == 0:
        basis[:, -1] = np.cos(np.pi * np.arange(length)) / math.sqrt(length)
    return basis


def slot_pieces(members, tokens, slots):
    pieces = []
    for member in range(members):
        first = member * tokens // PW
        for slot in range(slots):
            start = max((first + slot) * PW, member * tokens)
            stop = min((first + slot + 1) * PW, (member + 1) * tokens)
            if start < stop:
                pieces.append((
                    member,
                    slot,
                    (start - member * tokens, stop - member * tokens),
                    (start - (first + slot) * PW, stop - (first + slot) * PW),
                ))
    return pieces


def filter_tables(members, tokens, slots):
    rows = np.zeros((members * slots * 4, 2 * LANES))
    row_basis = real_basis(H)
    for member in range(members):
        first = member * tokens // PW
        for slot in range(slots):
            for dy in range(2):
                for dx in range(2):
                    if first + slot < PH:
                        rows[((member * slots + slot) * 2 + dy) * 2 + dx, :H] = row_basis[
                            2 * (first + slot) + dy
                        ]
    cols = np.zeros((2 * LANES, 2 * LANES))
    col_basis = real_basis(W)
    for dx in range(2):
        cols[dx * LANES : dx * LANES + PW, :W] = col_basis[dx::2]
    parts = []
    for table in (rows, cols):
        high = table.astype(np.float32).astype(ml_dtypes.bfloat16)
        low = (table - high.astype(np.float64)).astype(np.float32).astype(ml_dtypes.bfloat16)
        parts += [high, low]
    return np.concatenate(parts, axis=0)


def split(value):
    high = value.astype(jnp.bfloat16)
    return high, (value - high.astype(jnp.float32)).astype(jnp.bfloat16)


def dot3(left, right, dims):
    def one(a, b):
        return lax.dot_general(a, b, (dims, ((), ())), preferred_element_type=jnp.float32)

    return one(left[0], right[0]) + (one(left[0], right[1]) + one(left[1], right[0]))


def exchange(source, target, send_sems, recv_sems, me, members):
    copies = []
    for step in range(1, members):
        peer = lax.rem(me + step, members)
        copy = pltpu.make_async_remote_copy(
            src_ref=source.at[peer],
            dst_ref=target.at[me],
            send_sem=send_sems.at[peer],
            recv_sem=recv_sems.at[me],
            device_id={"seq": peer},
            device_id_type=MESH,
        )
        copy.start()
        copies.append(copy)
    target[me] = source[me]
    return copies


def receive(source, target, send_sems, recv_sems, me, members):
    for step in range(1, members):
        peer = lax.rem(me + members - step, members)
        pltpu.make_async_remote_copy(
            src_ref=source.at[peer],
            dst_ref=target.at[peer],
            send_sem=send_sems.at[peer],
            recv_sem=recv_sems.at[peer],
            device_id={"seq": peer},
            device_id_type=MESH,
        ).wait_recv()


def step_kernel(
    members,
    tokens,
    slots,
    hidden_hbm,
    weight_hbm,
    table_hbm,
    modulation_hbm,
    latent_hbm,
    residual_ref,
    bias_ref,
    gain_ref,
    cut_rows_ref,
    cut_cols_ref,
    skip_ref,
    step_ref,
    velocity_ref,
    next_ref,
    hidden_ref,
    weight_ref,
    table_ref,
    modulation_ref,
    latent_ref,
    sent,
    got,
    back,
    home,
    slotted,
    low_ref,
    row_high,
    row_low,
    col_high,
    col_low,
    final_ref,
    load_sems,
    send_sems,
    recv_sems,
    back_send_sems,
    back_recv_sems,
):
    me = lax.axis_index("seq")
    loads = [
        pltpu.make_async_copy(source, target, load_sems.at[place])
        for place, (source, target) in enumerate((
            (table_hbm, table_ref),
            (hidden_hbm, hidden_ref),
            (weight_hbm, weight_ref),
            (modulation_hbm, modulation_ref),
            (latent_hbm, latent_ref),
        ))
    ]
    barrier = pltpu.get_barrier_semaphore()
    for step in range(1, members):
        peer = lax.rem(me + step, members)
        pl.semaphore_signal(barrier, inc=1, device_id={"seq": peer}, device_id_type=MESH)
    for load in loads:
        load.start()
    for channel in range(members):
        sent[channel, :, :tokens] = residual_ref[4 * channel : 4 * channel + 4, :]
    pl.semaphore_wait(barrier, members - 1)
    sends = exchange(sent, got, send_sems, recv_sems, me, members)

    pieces = slot_pieces(members, tokens, slots)
    slotted[...] = jnp.zeros_like(slotted)
    span = members * slots * 4
    wide = 2 * LANES
    loads[0].wait()
    frequency = (lax.broadcasted_iota(jnp.int32, (1, wide), 1) + 1) // 2
    for base, depth, cut, high_ref, low_part_ref in (
        (0, span, cut_rows_ref[0], row_high, row_low),
        (2 * span, wide, cut_cols_ref[0], col_high, col_low),
    ):
        high = table_ref[base : base + depth, :]
        low = table_ref[base + depth : base + 2 * depth, :]
        kept = (frequency <= cut).astype(jnp.float32).astype(jnp.bfloat16)
        matrix = dot3((high * kept, low * kept), (high, low), ((1,), (1,)))
        high_ref[...], low_part_ref[...] = split(matrix)

    loads[1].wait()
    width = hidden_ref.shape[1]

    def moment_step(index, carry):
        total, squares = carry
        start = pl.multiple_of(index * CHUNK, CHUNK)
        values = hidden_ref[:, pl.ds(start, CHUNK)].astype(jnp.float32)
        for lane in range(0, CHUNK, LANES):
            part = values[:, lane : lane + LANES]
            total = total + part
            squares = squares + part * part
        return total, squares

    zeros = jnp.zeros((tokens, LANES), jnp.float32)
    total, squares = lax.fori_loop(0, width // CHUNK, moment_step, (zeros, zeros))
    average = jnp.sum(total, axis=1, keepdims=True) / D
    second = jnp.sum(squares, axis=1, keepdims=True) / D
    scale_inv = lax.rsqrt(second - average * average + EPSILON)

    receive(sent, got, send_sems, recv_sems, me, members)
    for member, slot, (begin, end), (first, last) in pieces:
        at = (member * slots + slot) * 4
        slotted[at : at + 4, first:last] = got[member, :, begin:end]
    data = slotted[...]
    even = lax.broadcasted_iota(jnp.int32, (span, LANES), 0) % 2 == 0
    nothing = jnp.zeros_like(data)
    spread = jnp.concatenate(
        [jnp.where(even, data, nothing), jnp.where(even, nothing, data)], axis=1
    )
    filtered = dot3((row_high[...], row_low[...]), split(spread), ((1,), (0,)))
    filtered = dot3(split(filtered), (col_high[...], col_low[...]), ((1,), (0,)))
    low_ref[...] = jnp.where(even, filtered[:, :LANES], filtered[:, LANES:])
    for member, slot, (begin, end), (first, last) in pieces:
        at = (member * slots + slot) * 4
        back[member, :, begin:end] = low_ref[at : at + 4, first:last]
    returns = exchange(back, home, back_send_sems, back_recv_sems, me, members)

    loads[2].wait()
    loads[3].wait()

    def head_step(index, carry):
        start = pl.multiple_of(index * CHUNK, CHUNK)
        values = hidden_ref[:, pl.ds(start, CHUNK)].astype(jnp.float32)
        gain = 1.0 + modulation_ref[1:2, pl.ds(start, CHUNK)]
        shift = modulation_ref[0:1, pl.ds(start, CHUNK)]
        normed = ((values - average) * scale_inv * gain + shift).astype(jnp.bfloat16)
        return carry + jnp.dot(
            normed, weight_ref[pl.ds(start, CHUNK), :], preferred_element_type=jnp.float32
        )

    rows = residual_ref.shape[0]
    head = lax.fori_loop(
        0, width // CHUNK, head_step, jnp.zeros((tokens, rows), jnp.float32)
    )
    square = (rows, rows)
    diagonal = lax.broadcasted_iota(jnp.int32, square, 0) == lax.broadcasted_iota(
        jnp.int32, square, 1
    )
    bias = jnp.sum(jnp.where(diagonal, bias_ref[...], 0.0), axis=1, keepdims=True)
    conditional = head.T + bias

    current = step_ref[0]
    last_full = jnp.int32(-1)
    for index in range(skip_ref.shape[0]):
        computed = (skip_ref[index] == 0) & (index <= current)
        last_full = jnp.where(computed, index, last_full)
    spacing = jnp.full((rows, 1), current - last_full, jnp.int32).astype(jnp.float32)
    gap_ratio = spacing / (spacing + 2.0)
    channels = gain_ref.shape[1]
    own = lax.broadcasted_iota(jnp.int32, (rows, channels), 0) // 4 == lax.broadcasted_iota(
        jnp.int32, (rows, channels), 1
    )
    low_gain = jnp.sum(jnp.where(own, gain_ref[0:1, :], 0.0), axis=1, keepdims=True)
    high_gain = jnp.sum(jnp.where(own, gain_ref[1:2, :], 0.0), axis=1, keepdims=True)
    w_low = low_gain * (1.0 + gap_ratio)
    w_high = high_gain * (1.0 - 0.5 * gap_ratio)
    now = jnp.full((rows, 1), current, jnp.int32)
    change = sigma_at(now + 1) - sigma_at(now)

    loads[4].wait()
    receive(back, home, back_send_sems, back_recv_sems, me, members)
    for channel in range(members):
        final_ref[4 * channel : 4 * channel + 4, :] = home[channel, :, :tokens]
    low_band = final_ref[...]
    high_band = residual_ref[...] - low_band
    velocity = conditional + GUIDE_EXTRA * (w_low * low_band + w_high * high_band)
    velocity_ref[...] = velocity
    next_ref[...] = latent_ref[...] + change * velocity
    for copy in sends + returns:
        copy.wait_send()


def body(
    hidden,
    modulation,
    head_weight,
    head_bias,
    residual,
    latent,
    band_gain,
    cut_rows,
    cut_cols,
    skip_flags,
    step_index,
):
    rows, tokens = residual.shape
    members = PH * PW // tokens
    slots = (tokens + PW - 2) // PW + 1
    owner_each = (
        lax.axis_size("mp") == 1
        and lax.axis_size("seq") == members
        and rows == 4 * members
        and members * slots * 4 == 2 * LANES
        and hidden.shape[1] % CHUNK == 0
    )
    if not owner_each:
        return gathered_body(
            hidden,
            modulation,
            head_weight,
            head_bias,
            residual,
            latent,
            band_gain,
            cut_rows,
            cut_cols,
            skip_flags,
            step_index,
        )
    table = jnp.asarray(filter_tables(members, tokens, slots))
    span = members * slots * 4
    wide = 2 * LANES
    padded = -(-tokens // LANES) * LANES
    block = pltpu.VMEM((members, 4, padded), jnp.float32)
    out = jax.ShapeDtypeStruct((rows, tokens), jnp.float32)
    vmem = pl.BlockSpec(memory_space=pltpu.VMEM)
    smem = pl.BlockSpec(memory_space=pltpu.SMEM)
    hbm = pl.BlockSpec(memory_space=pl.ANY)
    return pl.pallas_call(
        functools.partial(step_kernel, members, tokens, slots),
        out_shape=(out, out),
        in_specs=[hbm] * 5 + [vmem] * 3 + [smem] * 4,
        out_specs=(vmem, vmem),
        scratch_shapes=[
            pltpu.VMEM(hidden.shape, hidden.dtype),
            pltpu.VMEM(head_weight.shape, head_weight.dtype),
            pltpu.VMEM(table.shape, table.dtype),
            pltpu.VMEM(modulation.shape, modulation.dtype),
            pltpu.VMEM(latent.shape, latent.dtype),
            block,
            block,
            block,
            block,
            pltpu.VMEM((span, LANES), jnp.float32),
            pltpu.VMEM((span, LANES), jnp.float32),
            pltpu.VMEM((span, span), jnp.bfloat16),
            pltpu.VMEM((span, span), jnp.bfloat16),
            pltpu.VMEM((wide, wide), jnp.bfloat16),
            pltpu.VMEM((wide, wide), jnp.bfloat16),
            pltpu.VMEM((rows, tokens), jnp.float32),
            pltpu.SemaphoreType.DMA((5,)),
            pltpu.SemaphoreType.DMA((members,)),
            pltpu.SemaphoreType.DMA((members,)),
            pltpu.SemaphoreType.DMA((members,)),
            pltpu.SemaphoreType.DMA((members,)),
        ],
        compiler_params=pltpu.CompilerParams(
            collective_id=0, has_side_effects=True, vmem_limit_bytes=48 * 1024 * 1024
        ),
        cost_estimate=pl.CostEstimate(
            flops=2 * tokens * hidden.shape[1] * rows,
            bytes_accessed=2 * hidden.size + 2 * head_weight.size,
            transcendentals=0,
        ),
    )(
        hidden,
        head_weight,
        table,
        modulation,
        latent,
        residual,
        head_bias.reshape(1, rows),
        band_gain,
        cut_rows,
        cut_cols,
        skip_flags,
        step_index,
    )


def solution(mesh):
    in_specs = (
        P(("groups", "seq"), "mp"),
        P("groups", "mp"),
        P("mp", None),
        P("mp"),
        P("mp", ("groups", "seq")),
        P("mp", ("groups", "seq")),
        P(None, "mp"),
        P("groups"),
        P("groups"),
        P("groups"),
        P("groups"),
    )
    out_specs = (P("mp", ("groups", "seq")), P("mp", ("groups", "seq")))
    return jax.shard_map(body, mesh=mesh, in_specs=in_specs, out_specs=out_specs, check_vma=False)
```

```python
import functools
import math

import jax
import jax.numpy as jnp
import ml_dtypes
import numpy as np
from jax import lax
from jax.experimental import pallas as pl
from jax.experimental.pallas import tpu as pltpu
from jax.sharding import PartitionSpec as P

D = 5120
H = 90
W = 160
PH = 45
PW = 80
NSTEP = 50


EPSILON = 1e-06
GUIDE_EXTRA = 4.0
SHIFT_FACTOR = 5.0
HIGHEST = lax.Precision.HIGHEST


def from_partner(value, axis, bit):
    mask = 2**bit
    pairs = [(source, source ^ mask) for source in range(lax.axis_size(axis))]
    return lax.ppermute(value, axis, pairs)


def sigma_at(step_number):
    remain = 1.0 - step_number.astype(jnp.float32) / NSTEP
    return SHIFT_FACTOR * remain / (1.0 + (SHIFT_FACTOR - 1.0) * remain)


def band_weights(skip_flags, step_index, band_gain):
    current = step_index[0]
    counter = jnp.arange(NSTEP, dtype=jnp.int32)
    computed = (skip_flags == 0) & (counter <= current)
    last_full = jnp.max(jnp.where(computed, counter, -1))
    spacing = (current - last_full).astype(jnp.float32)
    gap_ratio = spacing / (spacing + 2.0)
    return (band_gain[0] * (1.0 + gap_ratio), band_gain[1] * (1.0 - 0.5 * gap_ratio))


def band_matrix(length, cutoff):
    counter = jnp.arange(length, dtype=jnp.int32)
    product = counter[:, None] * counter[None, :] % length
    angles = 2.0 * math.pi / length * product.astype(jnp.float32)
    cosine = jnp.cos(angles)
    sine_table = jnp.sin(angles)
    kept_modes = (jnp.minimum(counter, length - counter) <= cutoff).astype(jnp.float32)
    summed = jnp.dot(cosine * kept_modes, cosine.T, precision=HIGHEST) + jnp.dot(
        sine_table * kept_modes, sine_table.T, precision=HIGHEST
    )
    return summed / length


def gathered_body(
    hidden,
    modulation,
    head_weight,
    head_bias,
    residual,
    latent,
    band_gain,
    cut_rows,
    cut_cols,
    skip_flags,
    step_index,
):
    values = hidden.astype(jnp.float32)
    moments = lax.psum((jnp.sum(values, axis=1), jnp.sum(values * values, axis=1)), "mp")
    average = moments[0] / D
    scale_inv = lax.rsqrt(moments[1] / D - average * average + EPSILON)
    normed = (
        (values - average[:, None]) * scale_inv[:, None] * (1.0 + modulation[1]) + modulation[0]
    ).astype(jnp.bfloat16)
    conditional = (
        lax.psum_scatter(
            lax.dot_general(
                head_weight, normed, (((0,), (1,)), ((), ())), preferred_element_type=jnp.float32
            ),
            "mp",
            scatter_dimension=0,
            tiled=True,
        )
        + head_bias[:, None]
    )
    local_rows = residual.shape[0]
    local_tokens = residual.shape[1]
    frame_tokens = PH * PW
    members = frame_tokens // local_tokens
    seq_index = lax.axis_index("seq")
    position = seq_index % members
    frame_index = seq_index // members
    frame_data = residual
    for section_bit in range(members.bit_length() - 1):
        partner = from_partner(frame_data, "seq", section_bit)
        upper_half = seq_index // (1 << section_bit) % 2 == 1
        frame_data = jnp.where(
            upper_half,
            jnp.concatenate([partner, frame_data], axis=1),
            jnp.concatenate([frame_data, partner], axis=1),
        )
    channels = local_rows // 4
    planes = (
        frame_data.reshape(channels, 2, 2, PH, PW).transpose(0, 3, 1, 4, 2).reshape(channels, H, W)
    )
    row_filter = band_matrix(H, cut_rows[frame_index])
    col_filter = band_matrix(W, cut_cols[frame_index])
    row_total = min(local_tokens // PW + 2, PH)
    first_row = jnp.minimum(position * local_tokens // PW, PH - row_total)
    row_part = lax.dynamic_slice_in_dim(row_filter, 2 * first_row, 2 * row_total, 0)
    partial_rows = jnp.einsum("ij,cjw->ciw", row_part, planes, precision=HIGHEST)
    low_rows = jnp.dot(
        partial_rows.reshape(channels * 2 * row_total, W), col_filter, precision=HIGHEST
    ).reshape(channels, 2 * row_total, W)
    low_tokens = (
        low_rows.reshape(channels, row_total, 2, PW, 2)
        .transpose(0, 2, 4, 1, 3)
        .reshape(local_rows, row_total * PW)
    )
    low_band = lax.dynamic_slice_in_dim(
        low_tokens, position * local_tokens - first_row * PW, local_tokens, 1
    )
    high_band = residual - low_band
    w_low, w_high = band_weights(skip_flags, step_index, band_gain)
    row_low = jnp.repeat(w_low, 4)[:, None]
    row_high = jnp.repeat(w_high, 4)[:, None]
    velocity = conditional + GUIDE_EXTRA * (row_low * low_band + row_high * high_band)
    current = step_index[0]
    latent_next = latent + (sigma_at(current + 1) - sigma_at(current)) * velocity
    return (velocity, latent_next)


LANES = 128
CHUNK = 1024
ROWS = 32
MESH = pl.DeviceIdType.MESH


def real_basis(length):
    place = np.arange(length)[:, None]
    column = np.arange(length)[None, :]
    frequency = (column + 1) // 2
    angle = 2.0 * np.pi * (place * frequency % length) / length
    basis = np.where(column % 2 == 1, np.cos(angle), np.sin(angle)) * math.sqrt(2.0 / length)
    basis[:, 0] = 1.0 / math.sqrt(length)
    if length % 2 == 0:
        basis[:, -1] = np.cos(np.pi * np.arange(length)) / math.sqrt(length)
    return basis


def slot_pieces(members, tokens, slots):
    pieces = []
    for member in range(members):
        first = member * tokens // PW
        for slot in range(slots):
            start = max((first + slot) * PW, member * tokens)
            stop = min((first + slot + 1) * PW, (member + 1) * tokens)
            if start < stop:
                pieces.append((
                    member,
                    slot,
                    (start - member * tokens, stop - member * tokens),
                    (start - (first + slot) * PW, stop - (first + slot) * PW),
                ))
    return pieces


def filter_tables(members, tokens, slots):
    rows = np.zeros((members * slots * 4, 2 * LANES))
    row_basis = real_basis(H)
    for member in range(members):
        first = member * tokens // PW
        for slot in range(slots):
            for dy in range(2):
                for dx in range(2):
                    if first + slot < PH:
                        rows[((member * slots + slot) * 2 + dy) * 2 + dx, :H] = row_basis[
                            2 * (first + slot) + dy
                        ]
    cols = np.zeros((2 * LANES, 2 * LANES))
    col_basis = real_basis(W)
    for dx in range(2):
        cols[dx * LANES : dx * LANES + PW, :W] = col_basis[dx::2]
    parts = []
    for table in (rows, cols):
        high = table.astype(np.float32).astype(ml_dtypes.bfloat16)
        low = (table - high.astype(np.float64)).astype(np.float32).astype(ml_dtypes.bfloat16)
        parts += [high, low]
    return np.concatenate(parts, axis=0)


def split(value):
    high = value.astype(jnp.bfloat16)
    return high, (value - high.astype(jnp.float32)).astype(jnp.bfloat16)


def dot3(left, right, dims):
    def one(a, b):
        return lax.dot_general(a, b, (dims, ((), ())), preferred_element_type=jnp.float32)

    return one(left[0], right[0]) + (one(left[0], right[1]) + one(left[1], right[0]))


def exchange(source, target, send_sems, recv_sems, me, members):
    copies = []
    for step in range(1, members):
        peer = lax.rem(me + step, members)
        copy = pltpu.make_async_remote_copy(
            src_ref=source.at[peer],
            dst_ref=target.at[me],
            send_sem=send_sems.at[peer],
            recv_sem=recv_sems.at[me],
            device_id={"seq": peer},
            device_id_type=MESH,
        )
        copy.start()
        copies.append(copy)
    target[me] = source[me]
    return copies


def receive(source, target, send_sems, recv_sems, me, members):
    for step in range(1, members):
        peer = lax.rem(me + members - step, members)
        pltpu.make_async_remote_copy(
            src_ref=source.at[peer],
            dst_ref=target.at[peer],
            send_sem=send_sems.at[peer],
            recv_sem=recv_sems.at[peer],
            device_id={"seq": peer},
            device_id_type=MESH,
        ).wait_recv()


def step_kernel(
    members,
    tokens,
    slots,
    hidden_hbm,
    weight_hbm,
    table_hbm,
    modulation_hbm,
    latent_hbm,
    residual_hbm,
    bias_hbm,
    gain_hbm,
    cut_rows_hbm,
    cut_cols_hbm,
    skip_hbm,
    step_hbm,
    velocity_ref,
    next_ref,
    hidden_ref,
    weight_ref,
    table_ref,
    modulation_ref,
    latent_ref,
    residual_ref,
    bias_ref,
    gain_ref,
    cut_rows_ref,
    cut_cols_ref,
    skip_ref,
    step_ref,
    sent,
    got,
    back,
    home,
    slotted,
    low_ref,
    row_high,
    row_low,
    col_high,
    col_low,
    final_ref,
    total_ref,
    square_ref,
    load_sems,
    send_sems,
    recv_sems,
    back_send_sems,
    back_recv_sems,
):
    me = lax.axis_index("seq")
    width = hidden_ref.shape[1]
    pairs = [
        (residual_hbm, residual_ref),
        (table_hbm, table_ref),
        (cut_rows_hbm, cut_rows_ref),
        (cut_cols_hbm, cut_cols_ref),
    ]
    quarter = width // 4
    for place in range(4):
        part = pl.ds(place * quarter, quarter)
        pairs.append((hidden_hbm.at[:, part], hidden_ref.at[:, part]))
    pairs += [
        (modulation_hbm, modulation_ref),
        (weight_hbm, weight_ref),
        (skip_hbm, skip_ref),
        (step_hbm, step_ref),
        (bias_hbm, bias_ref),
        (gain_hbm, gain_ref),
        (latent_hbm, latent_ref),
    ]
    loads = [
        pltpu.make_async_copy(source, target, load_sems.at[place])
        for place, (source, target) in enumerate(pairs)
    ]
    loads[0].start()
    barrier = pltpu.get_barrier_semaphore()
    for step in range(1, members):
        peer = lax.rem(me + step, members)
        pl.semaphore_signal(barrier, inc=1, device_id={"seq": peer}, device_id_type=MESH)
    for load in loads[1:]:
        load.start()
    loads[0].wait()
    for channel in range(members):
        sent[channel, :, :tokens] = residual_ref[4 * channel : 4 * channel + 4, :]
    pl.semaphore_wait(barrier, members - 1)
    sends = exchange(sent, got, send_sems, recv_sems, me, members)

    pieces = slot_pieces(members, tokens, slots)
    slotted[...] = jnp.zeros_like(slotted)
    span = members * slots * 4
    wide = 2 * LANES
    for load in loads[1:4]:
        load.wait()
    frequency = (lax.broadcasted_iota(jnp.int32, (1, wide), 1) + 1) // 2
    for base, depth, cut, high_ref, low_part_ref in (
        (0, span, cut_rows_ref[0], row_high, row_low),
        (2 * span, wide, cut_cols_ref[0], col_high, col_low),
    ):
        high = table_ref[base : base + depth, :]
        low = table_ref[base + depth : base + 2 * depth, :]
        kept = (frequency <= cut).astype(jnp.float32).astype(jnp.bfloat16)
        matrix = dot3((high * kept, low * kept), (high, low), ((1,), (1,)))
        high_ref[...], low_part_ref[...] = split(matrix)

    for load in loads[4:8]:
        load.wait()

    def moment_rows(rows):
        total = squares = None
        for lane in range(0, width, LANES):
            part = hidden_ref[rows, lane : lane + LANES].astype(jnp.float32)
            total = part if total is None else total + part
            squares = part * part if squares is None else squares + part * part
        total_ref[rows, :] = total
        square_ref[rows, :] = squares

    def moment_step(index, carry):
        moment_rows(pl.ds(pl.multiple_of(index * ROWS, ROWS), ROWS))
        return carry

    lax.fori_loop(0, tokens // ROWS, moment_step, 0)
    if tokens % ROWS:
        moment_rows(slice(tokens // ROWS * ROWS, tokens))
    average = jnp.sum(total_ref[...], axis=1, keepdims=True) / D
    second = jnp.sum(square_ref[...], axis=1, keepdims=True) / D
    scale_inv = lax.rsqrt(second - average * average + EPSILON)
    total_ref[...] = jnp.broadcast_to(average, total_ref.shape)
    square_ref[...] = jnp.broadcast_to(scale_inv, square_ref.shape)

    receive(sent, got, send_sems, recv_sems, me, members)
    for member, slot, (begin, end), (first, last) in pieces:
        at = (member * slots + slot) * 4
        slotted[at : at + 4, first:last] = got[member, :, begin:end]
    data = slotted[...]
    even = lax.broadcasted_iota(jnp.int32, (span, LANES), 0) % 2 == 0
    nothing = jnp.zeros_like(data)
    spread = jnp.concatenate(
        [jnp.where(even, data, nothing), jnp.where(even, nothing, data)], axis=1
    )
    filtered = dot3((row_high[...], row_low[...]), split(spread), ((1,), (0,)))
    filtered = dot3(split(filtered), (col_high[...], col_low[...]), ((1,), (0,)))
    low_ref[...] = jnp.where(even, filtered[:, :LANES], filtered[:, LANES:])
    for member, slot, (begin, end), (first, last) in pieces:
        at = (member * slots + slot) * 4
        back[member, :, begin:end] = low_ref[at : at + 4, first:last]
    returns = exchange(back, home, back_send_sems, back_recv_sems, me, members)

    for load in loads[8:]:
        load.wait()

    def head_step(index, carry):
        start = pl.multiple_of(index * CHUNK, CHUNK)
        average = total_ref[...]
        scale_inv = square_ref[...]
        parts = []
        for lane in range(0, CHUNK, LANES):
            at = pl.ds(pl.multiple_of(start + lane, LANES), LANES)
            values = hidden_ref[:, at].astype(jnp.float32)
            gain = 1.0 + modulation_ref[1:2, at]
            shift = modulation_ref[0:1, at]
            parts.append(
                ((values - average) * scale_inv * gain + shift).astype(jnp.bfloat16)
            )
        return carry + lax.dot_general(
            jnp.concatenate(parts, axis=1),
            weight_ref[:, pl.ds(start, CHUNK)],
            (((1,), (1,)), ((), ())),
            preferred_element_type=jnp.float32,
        )

    rows = residual_ref.shape[0]
    head = lax.fori_loop(
        0, width // CHUNK, head_step, jnp.zeros((tokens, rows), jnp.float32)
    )
    square = (rows, rows)
    diagonal = lax.broadcasted_iota(jnp.int32, square, 0) == lax.broadcasted_iota(
        jnp.int32, square, 1
    )
    bias = jnp.sum(jnp.where(diagonal, bias_ref[...], 0.0), axis=1, keepdims=True)
    conditional = head.T + bias

    current = step_ref[0]
    last_full = jnp.int32(-1)
    for index in range(skip_ref.shape[0]):
        computed = (skip_ref[index] == 0) & (index <= current)
        last_full = jnp.where(computed, index, last_full)
    spacing = jnp.full((rows, 1), current - last_full, jnp.int32).astype(jnp.float32)
    gap_ratio = spacing / (spacing + 2.0)
    channels = gain_ref.shape[1]
    own = lax.broadcasted_iota(jnp.int32, (rows, channels), 0) // 4 == lax.broadcasted_iota(
        jnp.int32, (rows, channels), 1
    )
    low_gain = jnp.sum(jnp.where(own, gain_ref[0:1, :], 0.0), axis=1, keepdims=True)
    high_gain = jnp.sum(jnp.where(own, gain_ref[1:2, :], 0.0), axis=1, keepdims=True)
    w_low = low_gain * (1.0 + gap_ratio)
    w_high = high_gain * (1.0 - 0.5 * gap_ratio)
    now = jnp.full((rows, 1), current, jnp.int32)
    change = sigma_at(now + 1) - sigma_at(now)

    receive(back, home, back_send_sems, back_recv_sems, me, members)
    for channel in range(members):
        final_ref[4 * channel : 4 * channel + 4, :] = home[channel, :, :tokens]
    low_band = final_ref[...]
    high_band = residual_ref[...] - low_band
    velocity = conditional + GUIDE_EXTRA * (w_low * low_band + w_high * high_band)
    velocity_ref[...] = velocity
    next_ref[...] = latent_ref[...] + change * velocity
    for copy in sends + returns:
        copy.wait_send()


def body(
    hidden,
    modulation,
    head_weight,
    head_bias,
    residual,
    latent,
    band_gain,
    cut_rows,
    cut_cols,
    skip_flags,
    step_index,
):
    rows, tokens = residual.shape
    members = PH * PW // tokens
    slots = (tokens + PW - 2) // PW + 1
    owner_each = (
        lax.axis_size("mp") == 1
        and lax.axis_size("seq") == members
        and rows == 4 * members
        and members * slots * 4 == 2 * LANES
        and hidden.shape[1] % CHUNK == 0
    )
    if not owner_each:
        return gathered_body(
            hidden,
            modulation,
            head_weight,
            head_bias,
            residual,
            latent,
            band_gain,
            cut_rows,
            cut_cols,
            skip_flags,
            step_index,
        )
    table = jnp.asarray(filter_tables(members, tokens, slots))
    span = members * slots * 4
    wide = 2 * LANES
    padded = -(-tokens // LANES) * LANES
    block = pltpu.VMEM((members, 4, padded), jnp.float32)
    out = jax.ShapeDtypeStruct((rows, tokens), jnp.float32)
    vmem = pl.BlockSpec(memory_space=pltpu.VMEM)
    operands = (
        hidden,
        head_weight.T,
        table,
        modulation,
        latent,
        residual,
        head_bias.reshape(1, rows),
        band_gain,
        cut_rows,
        cut_cols,
        skip_flags,
        step_index,
    )
    scalars = 4
    return pl.pallas_call(
        functools.partial(step_kernel, members, tokens, slots),
        out_shape=(out, out),
        in_specs=[pl.BlockSpec(memory_space=pltpu.HBM)] * len(operands),
        out_specs=(vmem, vmem),
        scratch_shapes=[pltpu.VMEM(each.shape, each.dtype) for each in operands[:-scalars]]
        + [pltpu.SMEM(each.shape, each.dtype) for each in operands[-scalars:]]
        + [
            block,
            block,
            block,
            block,
            pltpu.VMEM((span, LANES), jnp.float32),
            pltpu.VMEM((span, LANES), jnp.float32),
            pltpu.VMEM((span, span), jnp.bfloat16),
            pltpu.VMEM((span, span), jnp.bfloat16),
            pltpu.VMEM((wide, wide), jnp.bfloat16),
            pltpu.VMEM((wide, wide), jnp.bfloat16),
            pltpu.VMEM((rows, tokens), jnp.float32),
            pltpu.VMEM((tokens, LANES), jnp.float32),
            pltpu.VMEM((tokens, LANES), jnp.float32),
            pltpu.SemaphoreType.DMA((len(operands) + 3,)),
            pltpu.SemaphoreType.DMA((members,)),
            pltpu.SemaphoreType.DMA((members,)),
            pltpu.SemaphoreType.DMA((members,)),
            pltpu.SemaphoreType.DMA((members,)),
        ],
        compiler_params=pltpu.CompilerParams(
            collective_id=0, has_side_effects=True, vmem_limit_bytes=60 * 1024 * 1024
        ),
        cost_estimate=pl.CostEstimate(
            flops=2 * tokens * hidden.shape[1] * rows,
            bytes_accessed=2 * hidden.size + 2 * head_weight.size,
            transcendentals=0,
        ),
    )(*operands)


def solution(mesh):
    in_specs = (
        P(("groups", "seq"), "mp"),
        P("groups", "mp"),
        P("mp", None),
        P("mp"),
        P("mp", ("groups", "seq")),
        P("mp", ("groups", "seq")),
        P(None, "mp"),
        P("groups"),
        P("groups"),
        P("groups"),
        P("groups"),
    )
    out_specs = (P("mp", ("groups", "seq")), P("mp", ("groups", "seq")))
    return jax.shard_map(body, mesh=mesh, in_specs=in_specs, out_specs=out_specs, check_vma=False)
```

```python
import functools
import math

import jax
import jax.numpy as jnp
import ml_dtypes
import numpy as np
from jax import lax
from jax.experimental import pallas as pl
from jax.experimental.pallas import tpu as pltpu
from jax.sharding import PartitionSpec as P

D = 5120
H = 90
W = 160
PH = 45
PW = 80
NSTEP = 50


EPSILON = 1e-06
GUIDE_EXTRA = 4.0
SHIFT_FACTOR = 5.0
HIGHEST = lax.Precision.HIGHEST


def from_partner(value, axis, bit):
    mask = 2**bit
    pairs = [(source, source ^ mask) for source in range(lax.axis_size(axis))]
    return lax.ppermute(value, axis, pairs)


def sigma_at(step_number):
    remain = 1.0 - step_number.astype(jnp.float32) / NSTEP
    return SHIFT_FACTOR * remain / (1.0 + (SHIFT_FACTOR - 1.0) * remain)


def band_weights(skip_flags, step_index, band_gain):
    current = step_index[0]
    counter = jnp.arange(NSTEP, dtype=jnp.int32)
    computed = (skip_flags == 0) & (counter <= current)
    last_full = jnp.max(jnp.where(computed, counter, -1))
    spacing = (current - last_full).astype(jnp.float32)
    gap_ratio = spacing / (spacing + 2.0)
    return (band_gain[0] * (1.0 + gap_ratio), band_gain[1] * (1.0 - 0.5 * gap_ratio))


def band_matrix(length, cutoff):
    counter = jnp.arange(length, dtype=jnp.int32)
    product = counter[:, None] * counter[None, :] % length
    angles = 2.0 * math.pi / length * product.astype(jnp.float32)
    cosine = jnp.cos(angles)
    sine_table = jnp.sin(angles)
    kept_modes = (jnp.minimum(counter, length - counter) <= cutoff).astype(jnp.float32)
    summed = jnp.dot(cosine * kept_modes, cosine.T, precision=HIGHEST) + jnp.dot(
        sine_table * kept_modes, sine_table.T, precision=HIGHEST
    )
    return summed / length


def gathered_body(
    hidden,
    modulation,
    head_weight,
    head_bias,
    residual,
    latent,
    band_gain,
    cut_rows,
    cut_cols,
    skip_flags,
    step_index,
):
    values = hidden.astype(jnp.float32)
    moments = lax.psum((jnp.sum(values, axis=1), jnp.sum(values * values, axis=1)), "mp")
    average = moments[0] / D
    scale_inv = lax.rsqrt(moments[1] / D - average * average + EPSILON)
    normed = (
        (values - average[:, None]) * scale_inv[:, None] * (1.0 + modulation[1]) + modulation[0]
    ).astype(jnp.bfloat16)
    conditional = (
        lax.psum_scatter(
            lax.dot_general(
                head_weight, normed, (((0,), (1,)), ((), ())), preferred_element_type=jnp.float32
            ),
            "mp",
            scatter_dimension=0,
            tiled=True,
        )
        + head_bias[:, None]
    )
    local_rows = residual.shape[0]
    local_tokens = residual.shape[1]
    frame_tokens = PH * PW
    members = frame_tokens // local_tokens
    seq_index = lax.axis_index("seq")
    position = seq_index % members
    frame_index = seq_index // members
    frame_data = residual
    for section_bit in range(members.bit_length() - 1):
        partner = from_partner(frame_data, "seq", section_bit)
        upper_half = seq_index // (1 << section_bit) % 2 == 1
        frame_data = jnp.where(
            upper_half,
            jnp.concatenate([partner, frame_data], axis=1),
            jnp.concatenate([frame_data, partner], axis=1),
        )
    channels = local_rows // 4
    planes = (
        frame_data.reshape(channels, 2, 2, PH, PW).transpose(0, 3, 1, 4, 2).reshape(channels, H, W)
    )
    row_filter = band_matrix(H, cut_rows[frame_index])
    col_filter = band_matrix(W, cut_cols[frame_index])
    row_total = min(local_tokens // PW + 2, PH)
    first_row = jnp.minimum(position * local_tokens // PW, PH - row_total)
    row_part = lax.dynamic_slice_in_dim(row_filter, 2 * first_row, 2 * row_total, 0)
    partial_rows = jnp.einsum("ij,cjw->ciw", row_part, planes, precision=HIGHEST)
    low_rows = jnp.dot(
        partial_rows.reshape(channels * 2 * row_total, W), col_filter, precision=HIGHEST
    ).reshape(channels, 2 * row_total, W)
    low_tokens = (
        low_rows.reshape(channels, row_total, 2, PW, 2)
        .transpose(0, 2, 4, 1, 3)
        .reshape(local_rows, row_total * PW)
    )
    low_band = lax.dynamic_slice_in_dim(
        low_tokens, position * local_tokens - first_row * PW, local_tokens, 1
    )
    high_band = residual - low_band
    w_low, w_high = band_weights(skip_flags, step_index, band_gain)
    row_low = jnp.repeat(w_low, 4)[:, None]
    row_high = jnp.repeat(w_high, 4)[:, None]
    velocity = conditional + GUIDE_EXTRA * (row_low * low_band + row_high * high_band)
    current = step_index[0]
    latent_next = latent + (sigma_at(current + 1) - sigma_at(current)) * velocity
    return (velocity, latent_next)


LANES = 128
CHUNK = 1024
ROWS = 32
MESH = pl.DeviceIdType.MESH


def real_basis(length):
    place = np.arange(length)[:, None]
    column = np.arange(length)[None, :]
    frequency = (column + 1) // 2
    angle = 2.0 * np.pi * (place * frequency % length) / length
    basis = np.where(column % 2 == 1, np.cos(angle), np.sin(angle)) * math.sqrt(2.0 / length)
    basis[:, 0] = 1.0 / math.sqrt(length)
    if length % 2 == 0:
        basis[:, -1] = np.cos(np.pi * np.arange(length)) / math.sqrt(length)
    return basis


def slot_pieces(members, tokens, slots):
    pieces = []
    for member in range(members):
        first = member * tokens // PW
        for slot in range(slots):
            start = max((first + slot) * PW, member * tokens)
            stop = min((first + slot + 1) * PW, (member + 1) * tokens)
            if start < stop:
                pieces.append((
                    member,
                    slot,
                    (start - member * tokens, stop - member * tokens),
                    (start - (first + slot) * PW, stop - (first + slot) * PW),
                ))
    return pieces


def filter_tables(members, tokens, slots):
    rows = np.zeros((members * slots * 4, 2 * LANES))
    row_basis = real_basis(H)
    for member in range(members):
        first = member * tokens // PW
        for slot in range(slots):
            for dy in range(2):
                for dx in range(2):
                    if first + slot < PH:
                        rows[((member * slots + slot) * 2 + dy) * 2 + dx, :H] = row_basis[
                            2 * (first + slot) + dy
                        ]
    cols = np.zeros((2 * LANES, 2 * LANES))
    col_basis = real_basis(W)
    for dx in range(2):
        cols[dx * LANES : dx * LANES + PW, :W] = col_basis[dx::2]
    parts = []
    for table in (rows, cols):
        high = table.astype(np.float32).astype(ml_dtypes.bfloat16)
        low = (table - high.astype(np.float64)).astype(np.float32).astype(ml_dtypes.bfloat16)
        parts += [high, low]
    return np.concatenate(parts, axis=0)


def split(value):
    high = value.astype(jnp.bfloat16)
    return high, (value - high.astype(jnp.float32)).astype(jnp.bfloat16)


def dot3(left, right, dims):
    def one(a, b):
        return lax.dot_general(a, b, (dims, ((), ())), preferred_element_type=jnp.float32)

    return one(left[0], right[0]) + (one(left[0], right[1]) + one(left[1], right[0]))


def exchange(source, target, send_sems, recv_sems, me, members):
    copies = []
    for step in range(1, members):
        peer = lax.rem(me + step, members)
        copy = pltpu.make_async_remote_copy(
            src_ref=source.at[peer],
            dst_ref=target.at[me],
            send_sem=send_sems.at[peer],
            recv_sem=recv_sems.at[me],
            device_id={"seq": peer},
            device_id_type=MESH,
        )
        copy.start()
        copies.append(copy)
    target[me] = source[me]
    return copies


def receive(source, target, send_sems, recv_sems, me, members):
    for step in range(1, members):
        peer = lax.rem(me + members - step, members)
        pltpu.make_async_remote_copy(
            src_ref=source.at[peer],
            dst_ref=target.at[peer],
            send_sem=send_sems.at[peer],
            recv_sem=recv_sems.at[peer],
            device_id={"seq": peer},
            device_id_type=MESH,
        ).wait_recv()


def step_kernel(
    members,
    tokens,
    slots,
    hidden_hbm,
    weight_hbm,
    table_hbm,
    modulation_hbm,
    latent_hbm,
    residual_hbm,
    bias_hbm,
    gain_hbm,
    number_hbm,
    velocity_ref,
    next_ref,
    hidden_ref,
    weight_ref,
    table_ref,
    modulation_ref,
    latent_ref,
    residual_ref,
    bias_ref,
    gain_ref,
    number_ref,
    sent,
    got,
    back,
    home,
    slotted,
    low_ref,
    row_high,
    row_low,
    col_high,
    col_low,
    final_ref,
    total_ref,
    square_ref,
    load_sems,
    send_sems,
    recv_sems,
    back_send_sems,
    back_recv_sems,
):
    me = lax.axis_index("seq")
    width = hidden_ref.shape[1]
    pairs = [
        (residual_hbm, residual_ref),
        (table_hbm, table_ref),
        (number_hbm, number_ref),
    ]
    quarter = width // 4
    for place in range(4):
        part = pl.ds(place * quarter, quarter)
        pairs.append((hidden_hbm.at[:, part], hidden_ref.at[:, part]))
    pairs += [
        (modulation_hbm, modulation_ref),
        (weight_hbm, weight_ref),
        (bias_hbm, bias_ref),
        (gain_hbm, gain_ref),
        (latent_hbm, latent_ref),
    ]
    loads = [
        pltpu.make_async_copy(source, target, load_sems.at[place])
        for place, (source, target) in enumerate(pairs)
    ]
    loads[0].start()
    barrier = pltpu.get_barrier_semaphore()
    for step in range(1, members):
        peer = lax.rem(me + step, members)
        pl.semaphore_signal(barrier, inc=1, device_id={"seq": peer}, device_id_type=MESH)
    for load in loads[1:]:
        load.start()
    loads[0].wait()
    for channel in range(members):
        sent[channel, :, :tokens] = residual_ref[4 * channel : 4 * channel + 4, :]
    pl.semaphore_wait(barrier, members - 1)
    sends = exchange(sent, got, send_sems, recv_sems, me, members)

    pieces = slot_pieces(members, tokens, slots)
    slotted[...] = jnp.zeros_like(slotted)
    span = members * slots * 4
    wide = 2 * LANES
    for load in loads[1:3]:
        load.wait()
    frequency = (lax.broadcasted_iota(jnp.int32, (1, wide), 1) + 1) // 2
    for base, depth, cut, high_ref, low_part_ref in (
        (0, span, number_ref[NSTEP + 1], row_high, row_low),
        (2 * span, wide, number_ref[NSTEP + 2], col_high, col_low),
    ):
        high = table_ref[base : base + depth, :]
        low = table_ref[base + depth : base + 2 * depth, :]
        kept = (frequency <= cut).astype(jnp.float32).astype(jnp.bfloat16)
        matrix = dot3((high * kept, low * kept), (high, low), ((1,), (1,)))
        high_ref[...], low_part_ref[...] = split(matrix)

    for load in loads[3:7]:
        load.wait()

    def moment_rows(rows):
        total = squares = None
        for lane in range(0, width, LANES):
            part = hidden_ref[rows, lane : lane + LANES].astype(jnp.float32)
            total = part if total is None else total + part
            squares = part * part if squares is None else squares + part * part
        total_ref[rows, :] = total
        square_ref[rows, :] = squares

    def moment_step(index, carry):
        moment_rows(pl.ds(pl.multiple_of(index * ROWS, ROWS), ROWS))
        return carry

    lax.fori_loop(0, tokens // ROWS, moment_step, 0)
    if tokens % ROWS:
        moment_rows(slice(tokens // ROWS * ROWS, tokens))
    average = jnp.sum(total_ref[...], axis=1, keepdims=True) / D
    second = jnp.sum(square_ref[...], axis=1, keepdims=True) / D
    scale_inv = lax.rsqrt(second - average * average + EPSILON)
    total_ref[...] = jnp.broadcast_to(average, total_ref.shape)
    square_ref[...] = jnp.broadcast_to(scale_inv, square_ref.shape)

    receive(sent, got, send_sems, recv_sems, me, members)
    for member, slot, (begin, end), (first, last) in pieces:
        at = (member * slots + slot) * 4
        slotted[at : at + 4, first:last] = got[member, :, begin:end]
    data = slotted[...]
    even = lax.broadcasted_iota(jnp.int32, (span, LANES), 0) % 2 == 0
    nothing = jnp.zeros_like(data)
    spread = jnp.concatenate(
        [jnp.where(even, data, nothing), jnp.where(even, nothing, data)], axis=1
    )
    filtered = dot3((row_high[...], row_low[...]), split(spread), ((1,), (0,)))
    filtered = dot3(split(filtered), (col_high[...], col_low[...]), ((1,), (0,)))
    low_ref[...] = jnp.where(even, filtered[:, :LANES], filtered[:, LANES:])
    for member, slot, (begin, end), (first, last) in pieces:
        at = (member * slots + slot) * 4
        back[member, :, begin:end] = low_ref[at : at + 4, first:last]
    returns = exchange(back, home, back_send_sems, back_recv_sems, me, members)

    for load in loads[7:]:
        load.wait()

    def head_step(index, carry):
        start = pl.multiple_of(index * CHUNK, CHUNK)
        average = total_ref[...]
        scale_inv = square_ref[...]
        parts = []
        for lane in range(0, CHUNK, LANES):
            at = pl.ds(pl.multiple_of(start + lane, LANES), LANES)
            values = hidden_ref[:, at].astype(jnp.float32)
            gain = 1.0 + modulation_ref[1:2, at]
            shift = modulation_ref[0:1, at]
            parts.append(
                ((values - average) * scale_inv * gain + shift).astype(jnp.bfloat16)
            )
        return carry + lax.dot_general(
            jnp.concatenate(parts, axis=1),
            weight_ref[:, pl.ds(start, CHUNK)],
            (((1,), (1,)), ((), ())),
            preferred_element_type=jnp.float32,
        )

    rows = residual_ref.shape[0]
    head = lax.fori_loop(
        0, width // CHUNK, head_step, jnp.zeros((tokens, rows), jnp.float32)
    )
    square = (rows, rows)
    diagonal = lax.broadcasted_iota(jnp.int32, square, 0) == lax.broadcasted_iota(
        jnp.int32, square, 1
    )
    bias = jnp.sum(jnp.where(diagonal, bias_ref[...], 0.0), axis=1, keepdims=True)
    conditional = head.T + bias

    current = number_ref[NSTEP]
    last_full = jnp.int32(-1)
    for index in range(NSTEP):
        computed = (number_ref[index] == 0) & (index <= current)
        last_full = jnp.where(computed, index, last_full)
    spacing = jnp.full((rows, 1), current - last_full, jnp.int32).astype(jnp.float32)
    gap_ratio = spacing / (spacing + 2.0)
    channels = gain_ref.shape[1]
    own = lax.broadcasted_iota(jnp.int32, (rows, channels), 0) // 4 == lax.broadcasted_iota(
        jnp.int32, (rows, channels), 1
    )
    low_gain = jnp.sum(jnp.where(own, gain_ref[0:1, :], 0.0), axis=1, keepdims=True)
    high_gain = jnp.sum(jnp.where(own, gain_ref[1:2, :], 0.0), axis=1, keepdims=True)
    w_low = low_gain * (1.0 + gap_ratio)
    w_high = high_gain * (1.0 - 0.5 * gap_ratio)
    now = jnp.full((rows, 1), current, jnp.int32)
    change = sigma_at(now + 1) - sigma_at(now)

    receive(back, home, back_send_sems, back_recv_sems, me, members)
    for channel in range(members):
        final_ref[4 * channel : 4 * channel + 4, :] = home[channel, :, :tokens]
    low_band = final_ref[...]
    high_band = residual_ref[...] - low_band
    velocity = conditional + GUIDE_EXTRA * (w_low * low_band + w_high * high_band)
    velocity_ref[...] = velocity
    next_ref[...] = latent_ref[...] + change * velocity
    for copy in sends + returns:
        copy.wait_send()


def hand_out(velocity_in, next_in, velocity_out, next_out, sems):
    copies = [
        pltpu.make_async_copy(velocity_in, velocity_out, sems.at[0]),
        pltpu.make_async_copy(next_in, next_out, sems.at[1]),
    ]
    for copy in copies:
        copy.start()
    for copy in copies:
        copy.wait()


def body(
    hidden,
    modulation,
    head_weight,
    head_bias,
    residual,
    latent,
    band_gain,
    cut_rows,
    cut_cols,
    skip_flags,
    step_index,
):
    rows, tokens = residual.shape
    members = PH * PW // tokens
    slots = (tokens + PW - 2) // PW + 1
    owner_each = (
        lax.axis_size("mp") == 1
        and lax.axis_size("seq") == members
        and rows == 4 * members
        and members * slots * 4 == 2 * LANES
        and hidden.shape[1] % CHUNK == 0
    )
    if not owner_each:
        return gathered_body(
            hidden,
            modulation,
            head_weight,
            head_bias,
            residual,
            latent,
            band_gain,
            cut_rows,
            cut_cols,
            skip_flags,
            step_index,
        )
    table = jnp.asarray(filter_tables(members, tokens, slots))
    span = members * slots * 4
    wide = 2 * LANES
    padded = -(-tokens // LANES) * LANES
    block = pltpu.VMEM((members, 4, padded), jnp.float32)
    out = jax.ShapeDtypeStruct((rows, tokens), jnp.float32)
    vmem = pl.BlockSpec(memory_space=pltpu.VMEM)
    numbers = jnp.pad(skip_flags, (0, 3))
    for place, number in enumerate((step_index, cut_rows, cut_cols)):
        numbers = numbers + jnp.pad(number, (NSTEP + place, 2 - place))
    operands = (
        hidden,
        head_weight.T,
        table,
        modulation,
        latent,
        residual,
        head_bias.reshape(1, rows),
        band_gain,
        numbers,
    )
    scalars = 1
    velocity, latent_next = pl.pallas_call(
        functools.partial(step_kernel, members, tokens, slots),
        out_shape=(out, out),
        in_specs=[pl.BlockSpec(memory_space=pltpu.HBM)] * len(operands),
        out_specs=(vmem, vmem),
        scratch_shapes=[pltpu.VMEM(each.shape, each.dtype) for each in operands[:-scalars]]
        + [pltpu.SMEM(each.shape, each.dtype) for each in operands[-scalars:]]
        + [
            block,
            block,
            block,
            block,
            pltpu.VMEM((span, LANES), jnp.float32),
            pltpu.VMEM((span, LANES), jnp.float32),
            pltpu.VMEM((span, span), jnp.bfloat16),
            pltpu.VMEM((span, span), jnp.bfloat16),
            pltpu.VMEM((wide, wide), jnp.bfloat16),
            pltpu.VMEM((wide, wide), jnp.bfloat16),
            pltpu.VMEM((rows, tokens), jnp.float32),
            pltpu.VMEM((tokens, LANES), jnp.float32),
            pltpu.VMEM((tokens, LANES), jnp.float32),
            pltpu.SemaphoreType.DMA((len(operands) + 3,)),
            pltpu.SemaphoreType.DMA((members,)),
            pltpu.SemaphoreType.DMA((members,)),
            pltpu.SemaphoreType.DMA((members,)),
            pltpu.SemaphoreType.DMA((members,)),
        ],
        compiler_params=pltpu.CompilerParams(
            collective_id=0, has_side_effects=True, vmem_limit_bytes=48 * 1024 * 1024
        ),
        cost_estimate=pl.CostEstimate(
            flops=2 * tokens * hidden.shape[1] * rows,
            bytes_accessed=2 * hidden.size + 2 * head_weight.size,
            transcendentals=0,
        ),
    )(*(pltpu.with_memory_space_constraint(each, pltpu.HBM) for each in operands))
    hbm = pl.BlockSpec(memory_space=pl.ANY)
    return pl.pallas_call(
        hand_out,
        out_shape=(out, out),
        in_specs=[hbm, hbm],
        out_specs=(hbm, hbm),
        scratch_shapes=[pltpu.SemaphoreType.DMA((2,))],
    )(velocity, latent_next)


def solution(mesh):
    in_specs = (
        P(("groups", "seq"), "mp"),
        P("groups", "mp"),
        P("mp", None),
        P("mp"),
        P("mp", ("groups", "seq")),
        P("mp", ("groups", "seq")),
        P(None, "mp"),
        P("groups"),
        P("groups"),
        P("groups"),
        P("groups"),
    )
    out_specs = (P("mp", ("groups", "seq")), P("mp", ("groups", "seq")))
    return jax.shard_map(body, mesh=mesh, in_specs=in_specs, out_specs=out_specs, check_vma=False)
```

```python
import functools
import math

import jax
import jax.numpy as jnp
import ml_dtypes
import numpy as np
from jax import lax
from jax.experimental import pallas as pl
from jax.experimental.pallas import tpu as pltpu
from jax.sharding import PartitionSpec as P

D = 5120
H = 90
W = 160
PH = 45
PW = 80
NSTEP = 50


EPSILON = 1e-06
GUIDE_EXTRA = 4.0
SHIFT_FACTOR = 5.0
HIGHEST = lax.Precision.HIGHEST


def from_partner(value, axis, bit):
    mask = 2**bit
    pairs = [(source, source ^ mask) for source in range(lax.axis_size(axis))]
    return lax.ppermute(value, axis, pairs)


def sigma_at(step_number):
    remain = 1.0 - step_number.astype(jnp.float32) / NSTEP
    return SHIFT_FACTOR * remain / (1.0 + (SHIFT_FACTOR - 1.0) * remain)


def band_weights(skip_flags, step_index, band_gain):
    current = step_index[0]
    counter = jnp.arange(NSTEP, dtype=jnp.int32)
    computed = (skip_flags == 0) & (counter <= current)
    last_full = jnp.max(jnp.where(computed, counter, -1))
    spacing = (current - last_full).astype(jnp.float32)
    gap_ratio = spacing / (spacing + 2.0)
    return (band_gain[0] * (1.0 + gap_ratio), band_gain[1] * (1.0 - 0.5 * gap_ratio))


def band_matrix(length, cutoff):
    counter = jnp.arange(length, dtype=jnp.int32)
    product = counter[:, None] * counter[None, :] % length
    angles = 2.0 * math.pi / length * product.astype(jnp.float32)
    cosine = jnp.cos(angles)
    sine_table = jnp.sin(angles)
    kept_modes = (jnp.minimum(counter, length - counter) <= cutoff).astype(jnp.float32)
    summed = jnp.dot(cosine * kept_modes, cosine.T, precision=HIGHEST) + jnp.dot(
        sine_table * kept_modes, sine_table.T, precision=HIGHEST
    )
    return summed / length


def gathered_body(
    hidden,
    modulation,
    head_weight,
    head_bias,
    residual,
    latent,
    band_gain,
    cut_rows,
    cut_cols,
    skip_flags,
    step_index,
):
    values = hidden.astype(jnp.float32)
    moments = lax.psum((jnp.sum(values, axis=1), jnp.sum(values * values, axis=1)), "mp")
    average = moments[0] / D
    scale_inv = lax.rsqrt(moments[1] / D - average * average + EPSILON)
    normed = (
        (values - average[:, None]) * scale_inv[:, None] * (1.0 + modulation[1]) + modulation[0]
    ).astype(jnp.bfloat16)
    conditional = (
        lax.psum_scatter(
            lax.dot_general(
                head_weight, normed, (((0,), (1,)), ((), ())), preferred_element_type=jnp.float32
            ),
            "mp",
            scatter_dimension=0,
            tiled=True,
        )
        + head_bias[:, None]
    )
    local_rows = residual.shape[0]
    local_tokens = residual.shape[1]
    frame_tokens = PH * PW
    members = frame_tokens // local_tokens
    seq_index = lax.axis_index("seq")
    position = seq_index % members
    frame_index = seq_index // members
    frame_data = residual
    for section_bit in range(members.bit_length() - 1):
        partner = from_partner(frame_data, "seq", section_bit)
        upper_half = seq_index // (1 << section_bit) % 2 == 1
        frame_data = jnp.where(
            upper_half,
            jnp.concatenate([partner, frame_data], axis=1),
            jnp.concatenate([frame_data, partner], axis=1),
        )
    channels = local_rows // 4
    planes = (
        frame_data.reshape(channels, 2, 2, PH, PW).transpose(0, 3, 1, 4, 2).reshape(channels, H, W)
    )
    row_filter = band_matrix(H, cut_rows[frame_index])
    col_filter = band_matrix(W, cut_cols[frame_index])
    row_total = min(local_tokens // PW + 2, PH)
    first_row = jnp.minimum(position * local_tokens // PW, PH - row_total)
    row_part = lax.dynamic_slice_in_dim(row_filter, 2 * first_row, 2 * row_total, 0)
    partial_rows = jnp.einsum("ij,cjw->ciw", row_part, planes, precision=HIGHEST)
    low_rows = jnp.dot(
        partial_rows.reshape(channels * 2 * row_total, W), col_filter, precision=HIGHEST
    ).reshape(channels, 2 * row_total, W)
    low_tokens = (
        low_rows.reshape(channels, row_total, 2, PW, 2)
        .transpose(0, 2, 4, 1, 3)
        .reshape(local_rows, row_total * PW)
    )
    low_band = lax.dynamic_slice_in_dim(
        low_tokens, position * local_tokens - first_row * PW, local_tokens, 1
    )
    high_band = residual - low_band
    w_low, w_high = band_weights(skip_flags, step_index, band_gain)
    row_low = jnp.repeat(w_low, 4)[:, None]
    row_high = jnp.repeat(w_high, 4)[:, None]
    velocity = conditional + GUIDE_EXTRA * (row_low * low_band + row_high * high_band)
    current = step_index[0]
    latent_next = latent + (sigma_at(current + 1) - sigma_at(current)) * velocity
    return (velocity, latent_next)


LANES = 128
CHUNK = 1024
ROWS = 32
MESH = pl.DeviceIdType.MESH


def real_basis(length):
    place = np.arange(length)[:, None]
    column = np.arange(length)[None, :]
    frequency = (column + 1) // 2
    angle = 2.0 * np.pi * (place * frequency % length) / length
    basis = np.where(column % 2 == 1, np.cos(angle), np.sin(angle)) * math.sqrt(2.0 / length)
    basis[:, 0] = 1.0 / math.sqrt(length)
    if length % 2 == 0:
        basis[:, -1] = np.cos(np.pi * np.arange(length)) / math.sqrt(length)
    return basis


def slot_pieces(members, tokens, slots):
    pieces = []
    for member in range(members):
        first = member * tokens // PW
        for slot in range(slots):
            start = max((first + slot) * PW, member * tokens)
            stop = min((first + slot + 1) * PW, (member + 1) * tokens)
            if start < stop:
                pieces.append((
                    member,
                    slot,
                    (start - member * tokens, stop - member * tokens),
                    (start - (first + slot) * PW, stop - (first + slot) * PW),
                ))
    return pieces


def filter_tables(members, tokens, slots):
    rows = np.zeros((members * slots * 4, 2 * LANES))
    row_basis = real_basis(H)
    for member in range(members):
        first = member * tokens // PW
        for slot in range(slots):
            for dy in range(2):
                for dx in range(2):
                    if first + slot < PH:
                        rows[((member * slots + slot) * 2 + dy) * 2 + dx, :H] = row_basis[
                            2 * (first + slot) + dy
                        ]
    cols = np.zeros((2 * LANES, 2 * LANES))
    col_basis = real_basis(W)
    for dx in range(2):
        cols[dx * LANES : dx * LANES + PW, :W] = col_basis[dx::2]
    parts = []
    for table in (rows, cols):
        high = table.astype(np.float32).astype(ml_dtypes.bfloat16)
        low = (table - high.astype(np.float64)).astype(np.float32).astype(ml_dtypes.bfloat16)
        parts += [high, low]
    return np.concatenate(parts, axis=0)


def split(value):
    high = value.astype(jnp.bfloat16)
    return high, (value - high.astype(jnp.float32)).astype(jnp.bfloat16)


def dot3(left, right, dims):
    def one(a, b):
        return lax.dot_general(a, b, (dims, ((), ())), preferred_element_type=jnp.float32)

    return one(left[0], right[0]) + (one(left[0], right[1]) + one(left[1], right[0]))


def exchange(source, target, send_sem, recv_sem, me, members):
    for step in sorted(range(1, members), key=lambda step: abs(step - members // 2)):
        peer = lax.rem(me + step, members)
        pltpu.make_async_remote_copy(
            src_ref=source.at[peer],
            dst_ref=target.at[me],
            send_sem=send_sem,
            recv_sem=recv_sem,
            device_id={"seq": peer},
            device_id_type=MESH,
        ).start()
    target[me] = source[me]


def wait_all(block_ref, sem, members):
    others = block_ref.at[pl.ds(0, members - 1)]
    pltpu.make_async_copy(others, others, sem).wait()


def step_kernel(
    members,
    tokens,
    slots,
    hidden_hbm,
    weight_hbm,
    table_hbm,
    modulation_hbm,
    residual_hbm,
    bias_hbm,
    gain_hbm,
    step_hbm,
    cut_rows_hbm,
    cut_cols_hbm,
    skip_hbm,
    conditional_ref,
    guided_ref,
    change_ref,
    hidden_ref,
    weight_ref,
    table_ref,
    modulation_ref,
    residual_ref,
    bias_ref,
    gain_ref,
    step_ref,
    cut_rows_ref,
    cut_cols_ref,
    skip_ref,
    sent,
    got,
    back,
    home,
    slotted,
    low_ref,
    row_high,
    row_low,
    col_high,
    col_low,
    final_ref,
    total_ref,
    square_ref,
    load_sems,
    send_sems,
    recv_sems,
):
    me = lax.axis_index("seq")
    width = hidden_ref.shape[1]
    pairs = [
        (residual_hbm, residual_ref),
        (table_hbm, table_ref),
        (cut_rows_hbm, cut_rows_ref),
        (cut_cols_hbm, cut_cols_ref),
        (step_hbm, step_ref),
        (skip_hbm, skip_ref),
    ]
    quarter = width // 4
    for place in range(4):
        part = pl.ds(place * quarter, quarter)
        pairs.append((hidden_hbm.at[:, part], hidden_ref.at[:, part]))
    pairs += [
        (modulation_hbm, modulation_ref),
        (weight_hbm, weight_ref),
        (bias_hbm, bias_ref),
        (gain_hbm, gain_ref),
    ]
    loads = [
        pltpu.make_async_copy(source, target, load_sems.at[place])
        for place, (source, target) in enumerate(pairs)
    ]
    loads[0].start()
    barrier = pltpu.get_barrier_semaphore()
    for step in range(1, members):
        peer = lax.rem(me + step, members)
        pl.semaphore_signal(barrier, inc=1, device_id={"seq": peer}, device_id_type=MESH)
    for load in loads[1:]:
        load.start()
    pieces = slot_pieces(members, tokens, slots)
    slotted[...] = jnp.zeros_like(slotted)
    span = members * slots * 4
    wide = 2 * LANES
    for load in loads[1:6]:
        load.wait()
    frequency = (lax.broadcasted_iota(jnp.int32, (1, wide), 1) + 1) // 2
    for base, depth, cut, high_ref, low_part_ref in (
        (0, span, cut_rows_ref[0], row_high, row_low),
        (2 * span, wide, cut_cols_ref[0], col_high, col_low),
    ):
        high = table_ref[base : base + depth, :]
        low = table_ref[base + depth : base + 2 * depth, :]
        kept = (frequency <= cut).astype(jnp.float32).astype(jnp.bfloat16)
        matrix = dot3((high * kept, low * kept), (high, low), ((1,), (1,)))
        high_ref[...], low_part_ref[...] = split(matrix)

    loads[0].wait()
    for channel in range(members):
        sent[channel, :, :tokens] = residual_ref[4 * channel : 4 * channel + 4, :]
    pl.semaphore_wait(barrier, members - 1)
    exchange(sent, got, send_sems.at[0], recv_sems.at[0], me, members)

    for load in loads[6:10]:
        load.wait()

    def moment_rows(rows):
        total = squares = None
        for lane in range(0, width, LANES):
            part = hidden_ref[rows, lane : lane + LANES].astype(jnp.float32)
            total = part if total is None else total + part
            squares = part * part if squares is None else squares + part * part
        total_ref[rows, :] = total
        square_ref[rows, :] = squares

    def moment_step(index, carry):
        moment_rows(pl.ds(pl.multiple_of(index * ROWS, ROWS), ROWS))
        return carry

    lax.fori_loop(0, tokens // ROWS, moment_step, 0)
    if tokens % ROWS:
        moment_rows(slice(tokens // ROWS * ROWS, tokens))
    average = jnp.sum(total_ref[...], axis=1, keepdims=True) / D
    second = jnp.sum(square_ref[...], axis=1, keepdims=True) / D
    scale_inv = lax.rsqrt(second - average * average + EPSILON)
    total_ref[...] = jnp.broadcast_to(average, total_ref.shape)
    square_ref[...] = jnp.broadcast_to(scale_inv, square_ref.shape)

    for load in loads[10:]:
        load.wait()

    def head_step(index, carry):
        start = pl.multiple_of(index * CHUNK, CHUNK)
        average = total_ref[...]
        scale_inv = square_ref[...]
        parts = []
        for lane in range(0, CHUNK, LANES):
            at = pl.ds(pl.multiple_of(start + lane, LANES), LANES)
            values = hidden_ref[:, at].astype(jnp.float32)
            gain = 1.0 + modulation_ref[1:2, at]
            shift = modulation_ref[0:1, at]
            parts.append(
                ((values - average) * scale_inv * gain + shift).astype(jnp.bfloat16)
            )
        return carry + lax.dot_general(
            jnp.concatenate(parts, axis=1),
            weight_ref[:, pl.ds(start, CHUNK)],
            (((1,), (1,)), ((), ())),
            preferred_element_type=jnp.float32,
        )

    rows = residual_ref.shape[0]
    chunks = width // CHUNK
    early = chunks * 2 // 5
    head = lax.fori_loop(0, early, head_step, jnp.zeros((tokens, rows), jnp.float32))

    wait_all(got, recv_sems.at[0], members)
    for member, slot, (begin, end), (first, last) in pieces:
        at = (member * slots + slot) * 4
        slotted[at : at + 4, first:last] = got[member, :, begin:end]
    data = slotted[...]
    even = lax.broadcasted_iota(jnp.int32, (span, LANES), 0) % 2 == 0
    nothing = jnp.zeros_like(data)
    spread = jnp.concatenate(
        [jnp.where(even, data, nothing), jnp.where(even, nothing, data)], axis=1
    )
    filtered = dot3((row_high[...], row_low[...]), split(spread), ((1,), (0,)))
    filtered = dot3(split(filtered), (col_high[...], col_low[...]), ((1,), (0,)))
    low_ref[...] = jnp.where(even, filtered[:, :LANES], filtered[:, LANES:])
    for member, slot, (begin, end), (first, last) in pieces:
        at = (member * slots + slot) * 4
        back[member, :, begin:end] = low_ref[at : at + 4, first:last]
    exchange(back, home, send_sems.at[1], recv_sems.at[1], me, members)

    head = lax.fori_loop(early, chunks, head_step, head)
    square = (rows, rows)
    diagonal = lax.broadcasted_iota(jnp.int32, square, 0) == lax.broadcasted_iota(
        jnp.int32, square, 1
    )
    bias = jnp.sum(jnp.where(diagonal, bias_ref[...], 0.0), axis=1, keepdims=True)
    conditional = head.T + bias

    current = step_ref[0]
    last_full = jnp.int32(-1)
    for index in range(NSTEP):
        computed = (skip_ref[index] == 0) & (index <= current)
        last_full = jnp.where(computed, index, last_full)
    spacing = jnp.full((rows, 1), current - last_full, jnp.int32).astype(jnp.float32)
    gap_ratio = spacing / (spacing + 2.0)
    channels = gain_ref.shape[1]
    own = lax.broadcasted_iota(jnp.int32, (rows, channels), 0) // 4 == lax.broadcasted_iota(
        jnp.int32, (rows, channels), 1
    )
    low_gain = jnp.sum(jnp.where(own, gain_ref[0:1, :], 0.0), axis=1, keepdims=True)
    high_gain = jnp.sum(jnp.where(own, gain_ref[1:2, :], 0.0), axis=1, keepdims=True)
    w_low = low_gain * (1.0 + gap_ratio)
    w_high = high_gain * (1.0 - 0.5 * gap_ratio)
    now = jnp.full((rows, 1), current, jnp.int32)
    change = sigma_at(now + 1) - sigma_at(now)

    conditional_ref[...] = conditional
    change_ref[...] = jnp.broadcast_to(change, change_ref.shape)
    wait_all(home, recv_sems.at[1], members)
    for channel in range(members):
        final_ref[4 * channel : 4 * channel + 4, :] = home[channel, :, :tokens]
    low_band = final_ref[...]
    high_band = residual_ref[...] - low_band
    guided_ref[...] = GUIDE_EXTRA * (w_low * low_band + w_high * high_band)
    wait_all(sent, send_sems.at[0], members)
    wait_all(back, send_sems.at[1], members)


def body(
    hidden,
    modulation,
    head_weight,
    head_bias,
    residual,
    latent,
    band_gain,
    cut_rows,
    cut_cols,
    skip_flags,
    step_index,
):
    rows, tokens = residual.shape
    members = PH * PW // tokens
    slots = (tokens + PW - 2) // PW + 1
    owner_each = (
        lax.axis_size("mp") == 1
        and lax.axis_size("seq") == members
        and rows == 4 * members
        and members * slots * 4 == 2 * LANES
        and hidden.shape[1] % CHUNK == 0
    )
    if not owner_each:
        return gathered_body(
            hidden,
            modulation,
            head_weight,
            head_bias,
            residual,
            latent,
            band_gain,
            cut_rows,
            cut_cols,
            skip_flags,
            step_index,
        )
    table = jnp.asarray(filter_tables(members, tokens, slots))
    span = members * slots * 4
    wide = 2 * LANES
    padded = -(-tokens // LANES) * LANES
    block = pltpu.VMEM((members, 4, padded), jnp.float32)
    out = jax.ShapeDtypeStruct((rows, tokens), jnp.float32)
    vmem = pl.BlockSpec(memory_space=pltpu.VMEM)
    operands = (
        hidden,
        head_weight.T,
        table,
        modulation,
        residual,
        head_bias.reshape(1, rows),
        band_gain,
        step_index,
        cut_rows,
        cut_cols,
        skip_flags,
    )
    scalars = 4
    conditional, guided, change = pl.pallas_call(
        functools.partial(step_kernel, members, tokens, slots),
        out_shape=(out, out, out),
        in_specs=[pl.BlockSpec(memory_space=pltpu.HBM)] * len(operands),
        out_specs=(vmem, vmem, vmem),
        scratch_shapes=[pltpu.VMEM(each.shape, each.dtype) for each in operands[:-scalars]]
        + [pltpu.SMEM(each.shape, each.dtype) for each in operands[-scalars:]]
        + [
            block,
            block,
            block,
            block,
            pltpu.VMEM((span, LANES), jnp.float32),
            pltpu.VMEM((span, LANES), jnp.float32),
            pltpu.VMEM((span, span), jnp.bfloat16),
            pltpu.VMEM((span, span), jnp.bfloat16),
            pltpu.VMEM((wide, wide), jnp.bfloat16),
            pltpu.VMEM((wide, wide), jnp.bfloat16),
            pltpu.VMEM((rows, tokens), jnp.float32),
            pltpu.VMEM((tokens, LANES), jnp.float32),
            pltpu.VMEM((tokens, LANES), jnp.float32),
            pltpu.SemaphoreType.DMA((len(operands) + 3,)),
            pltpu.SemaphoreType.DMA((2,)),
            pltpu.SemaphoreType.DMA((2,)),
        ],
        compiler_params=pltpu.CompilerParams(
            collective_id=0, has_side_effects=True, vmem_limit_bytes=48 * 1024 * 1024
        ),
        cost_estimate=pl.CostEstimate(
            flops=2 * tokens * hidden.shape[1] * rows,
            bytes_accessed=2 * hidden.size + 2 * head_weight.size,
            transcendentals=0,
        ),
    )(*(each if each.size == 1 else pltpu.with_memory_space_constraint(each, pltpu.HBM)
            for each in operands))
    velocity = conditional + guided
    return (velocity, latent + change * velocity)


def solution(mesh):
    in_specs = (
        P(("groups", "seq"), "mp"),
        P("groups", "mp"),
        P("mp", None),
        P("mp"),
        P("mp", ("groups", "seq")),
        P("mp", ("groups", "seq")),
        P(None, "mp"),
        P("groups"),
        P("groups"),
        P("groups"),
        P("groups"),
    )
    out_specs = (P("mp", ("groups", "seq")), P("mp", ("groups", "seq")))
    return jax.shard_map(body, mesh=mesh, in_specs=in_specs, out_specs=out_specs, check_vma=False)
```

```python
import functools
import math

import jax
import jax.numpy as jnp
import ml_dtypes
import numpy as np
from jax import lax
from jax.experimental import pallas as pl
from jax.experimental.pallas import tpu as pltpu
from jax.sharding import PartitionSpec as P

D = 5120
H = 90
W = 160
PH = 45
PW = 80
NSTEP = 50


EPSILON = 1e-06
GUIDE_EXTRA = 4.0
SHIFT_FACTOR = 5.0
HIGHEST = lax.Precision.HIGHEST


def from_partner(value, axis, bit):
    mask = 2**bit
    pairs = [(source, source ^ mask) for source in range(lax.axis_size(axis))]
    return lax.ppermute(value, axis, pairs)


def sigma_at(step_number):
    remain = 1.0 - step_number.astype(jnp.float32) / NSTEP
    return SHIFT_FACTOR * remain / (1.0 + (SHIFT_FACTOR - 1.0) * remain)


def band_weights(skip_flags, step_index, band_gain):
    current = step_index[0]
    counter = jnp.arange(NSTEP, dtype=jnp.int32)
    computed = (skip_flags == 0) & (counter <= current)
    last_full = jnp.max(jnp.where(computed, counter, -1))
    spacing = (current - last_full).astype(jnp.float32)
    gap_ratio = spacing / (spacing + 2.0)
    return (band_gain[0] * (1.0 + gap_ratio), band_gain[1] * (1.0 - 0.5 * gap_ratio))


def band_matrix(length, cutoff):
    counter = jnp.arange(length, dtype=jnp.int32)
    product = counter[:, None] * counter[None, :] % length
    angles = 2.0 * math.pi / length * product.astype(jnp.float32)
    cosine = jnp.cos(angles)
    sine_table = jnp.sin(angles)
    kept_modes = (jnp.minimum(counter, length - counter) <= cutoff).astype(jnp.float32)
    summed = jnp.dot(cosine * kept_modes, cosine.T, precision=HIGHEST) + jnp.dot(
        sine_table * kept_modes, sine_table.T, precision=HIGHEST
    )
    return summed / length


def gathered_body(
    hidden,
    modulation,
    head_weight,
    head_bias,
    residual,
    latent,
    band_gain,
    cut_rows,
    cut_cols,
    skip_flags,
    step_index,
):
    values = hidden.astype(jnp.float32)
    moments = lax.psum((jnp.sum(values, axis=1), jnp.sum(values * values, axis=1)), "mp")
    average = moments[0] / D
    scale_inv = lax.rsqrt(moments[1] / D - average * average + EPSILON)
    normed = (
        (values - average[:, None]) * scale_inv[:, None] * (1.0 + modulation[1]) + modulation[0]
    ).astype(jnp.bfloat16)
    conditional = (
        lax.psum_scatter(
            lax.dot_general(
                head_weight, normed, (((0,), (1,)), ((), ())), preferred_element_type=jnp.float32
            ),
            "mp",
            scatter_dimension=0,
            tiled=True,
        )
        + head_bias[:, None]
    )
    local_rows = residual.shape[0]
    local_tokens = residual.shape[1]
    frame_tokens = PH * PW
    members = frame_tokens // local_tokens
    seq_index = lax.axis_index("seq")
    position = seq_index % members
    frame_index = seq_index // members
    frame_data = residual
    for section_bit in range(members.bit_length() - 1):
        partner = from_partner(frame_data, "seq", section_bit)
        upper_half = seq_index // (1 << section_bit) % 2 == 1
        frame_data = jnp.where(
            upper_half,
            jnp.concatenate([partner, frame_data], axis=1),
            jnp.concatenate([frame_data, partner], axis=1),
        )
    channels = local_rows // 4
    planes = (
        frame_data.reshape(channels, 2, 2, PH, PW).transpose(0, 3, 1, 4, 2).reshape(channels, H, W)
    )
    row_filter = band_matrix(H, cut_rows[frame_index])
    col_filter = band_matrix(W, cut_cols[frame_index])
    row_total = min(local_tokens // PW + 2, PH)
    first_row = jnp.minimum(position * local_tokens // PW, PH - row_total)
    row_part = lax.dynamic_slice_in_dim(row_filter, 2 * first_row, 2 * row_total, 0)
    partial_rows = jnp.einsum("ij,cjw->ciw", row_part, planes, precision=HIGHEST)
    low_rows = jnp.dot(
        partial_rows.reshape(channels * 2 * row_total, W), col_filter, precision=HIGHEST
    ).reshape(channels, 2 * row_total, W)
    low_tokens = (
        low_rows.reshape(channels, row_total, 2, PW, 2)
        .transpose(0, 2, 4, 1, 3)
        .reshape(local_rows, row_total * PW)
    )
    low_band = lax.dynamic_slice_in_dim(
        low_tokens, position * local_tokens - first_row * PW, local_tokens, 1
    )
    high_band = residual - low_band
    w_low, w_high = band_weights(skip_flags, step_index, band_gain)
    row_low = jnp.repeat(w_low, 4)[:, None]
    row_high = jnp.repeat(w_high, 4)[:, None]
    velocity = conditional + GUIDE_EXTRA * (row_low * low_band + row_high * high_band)
    current = step_index[0]
    latent_next = latent + (sigma_at(current + 1) - sigma_at(current)) * velocity
    return (velocity, latent_next)


LANES = 128
CHUNK = 1024
ROWS = 32
MESH = pl.DeviceIdType.MESH


def real_basis(length):
    place = np.arange(length)[:, None]
    column = np.arange(length)[None, :]
    frequency = (column + 1) // 2
    angle = 2.0 * np.pi * (place * frequency % length) / length
    basis = np.where(column % 2 == 1, np.cos(angle), np.sin(angle)) * math.sqrt(2.0 / length)
    basis[:, 0] = 1.0 / math.sqrt(length)
    if length % 2 == 0:
        basis[:, -1] = np.cos(np.pi * np.arange(length)) / math.sqrt(length)
    return basis


def slot_pieces(members, tokens, slots):
    pieces = []
    for member in range(members):
        first = member * tokens // PW
        for slot in range(slots):
            start = max((first + slot) * PW, member * tokens)
            stop = min((first + slot + 1) * PW, (member + 1) * tokens)
            if start < stop:
                pieces.append((
                    member,
                    slot,
                    (start - member * tokens, stop - member * tokens),
                    (start - (first + slot) * PW, stop - (first + slot) * PW),
                ))
    return pieces


def filter_tables(members, tokens, slots):
    rows = np.zeros((members * slots * 4, 2 * LANES))
    row_basis = real_basis(H)
    for member in range(members):
        first = member * tokens // PW
        for slot in range(slots):
            for dy in range(2):
                for dx in range(2):
                    if first + slot < PH:
                        rows[((member * slots + slot) * 2 + dy) * 2 + dx, :H] = row_basis[
                            2 * (first + slot) + dy
                        ]
    cols = np.zeros((2 * LANES, 2 * LANES))
    col_basis = real_basis(W)
    for dx in range(2):
        cols[dx * LANES : dx * LANES + PW, :W] = col_basis[dx::2]
    parts = []
    for table in (rows, cols):
        high = table.astype(np.float32).astype(ml_dtypes.bfloat16)
        low = (table - high.astype(np.float64)).astype(np.float32).astype(ml_dtypes.bfloat16)
        parts += [high, low]
    return np.concatenate(parts, axis=0)


def split(value):
    high = value.astype(jnp.bfloat16)
    return high, (value - high.astype(jnp.float32)).astype(jnp.bfloat16)


def dot3(left, right, dims):
    def one(a, b):
        return lax.dot_general(a, b, (dims, ((), ())), preferred_element_type=jnp.float32)

    return one(left[0], right[0]) + (one(left[0], right[1]) + one(left[1], right[0]))


def exchange(source, target, send_sem, recv_sem, me, members):
    for step in sorted(range(1, members), key=lambda step: abs(step - members // 2)):
        peer = lax.rem(me + step, members)
        pltpu.make_async_remote_copy(
            src_ref=source.at[peer],
            dst_ref=target.at[me],
            send_sem=send_sem,
            recv_sem=recv_sem,
            device_id={"seq": peer},
            device_id_type=MESH,
        ).start()
    target[me] = source[me]


def wait_all(block_ref, sem, members):
    others = block_ref.at[pl.ds(0, members - 1)]
    pltpu.make_async_copy(others, others, sem).wait()


def step_kernel(
    members,
    tokens,
    slots,
    hidden_hbm,
    weight_hbm,
    table_hbm,
    modulation_hbm,
    residual_hbm,
    bias_hbm,
    gain_hbm,
    step_hbm,
    cut_rows_hbm,
    cut_cols_hbm,
    skip_hbm,
    conditional_ref,
    guided_ref,
    change_ref,
    hidden_ref,
    weight_ref,
    table_ref,
    modulation_ref,
    residual_ref,
    bias_ref,
    gain_ref,
    step_ref,
    cut_rows_ref,
    cut_cols_ref,
    skip_ref,
    sent,
    got,
    back,
    home,
    slotted,
    low_ref,
    row_high,
    row_low,
    col_high,
    col_low,
    final_ref,
    total_ref,
    square_ref,
    scaled_ref,
    shifted_ref,
    load_sems,
    send_sems,
    recv_sems,
):
    me = lax.axis_index("seq")
    width = hidden_ref.shape[1]
    pairs = [
        (residual_hbm, residual_ref),
        (table_hbm, table_ref),
        (cut_rows_hbm, cut_rows_ref),
        (cut_cols_hbm, cut_cols_ref),
        (step_hbm, step_ref),
        (skip_hbm, skip_ref),
    ]
    quarter = width // 4
    for place in range(4):
        part = pl.ds(place * quarter, quarter)
        pairs.append((hidden_hbm.at[:, part], hidden_ref.at[:, part]))
    pairs += [
        (modulation_hbm, modulation_ref),
        (weight_hbm, weight_ref),
        (bias_hbm, bias_ref),
        (gain_hbm, gain_ref),
    ]
    loads = [
        pltpu.make_async_copy(source, target, load_sems.at[place])
        for place, (source, target) in enumerate(pairs)
    ]
    loads[0].start()
    barrier = pltpu.get_barrier_semaphore()
    for step in range(1, members):
        peer = lax.rem(me + step, members)
        pl.semaphore_signal(barrier, inc=1, device_id={"seq": peer}, device_id_type=MESH)
    for load in loads[1:]:
        load.start()
    pieces = slot_pieces(members, tokens, slots)
    slotted[...] = jnp.zeros_like(slotted)
    span = members * slots * 4
    wide = 2 * LANES
    for load in loads[1:6]:
        load.wait()
    frequency = (lax.broadcasted_iota(jnp.int32, (1, wide), 1) + 1) // 2
    for base, depth, cut, high_ref, low_part_ref in (
        (0, span, cut_rows_ref[0], row_high, row_low),
        (2 * span, wide, cut_cols_ref[0], col_high, col_low),
    ):
        high = table_ref[base : base + depth, :]
        low = table_ref[base + depth : base + 2 * depth, :]
        kept = (frequency <= cut).astype(jnp.float32).astype(jnp.bfloat16)
        matrix = dot3((high * kept, low * kept), (high, low), ((1,), (1,)))
        high_ref[...], low_part_ref[...] = split(matrix)

    loads[0].wait()
    for channel in range(members):
        sent[channel, :, :tokens] = residual_ref[4 * channel : 4 * channel + 4, :]
    pl.semaphore_wait(barrier, members - 1)
    exchange(sent, got, send_sems.at[0], recv_sems.at[0], me, members)

    for load in loads[6:]:
        load.wait()
    for each in (total_ref, square_ref, scaled_ref, shifted_ref):
        each[...] = jnp.zeros_like(each)

    def lane_sum(values):
        return sum(values[:, lane : lane + LANES] for lane in range(0, CHUNK, LANES))

    def head_step(index, carry):
        start = pl.multiple_of(index * CHUNK, CHUNK)
        at = pl.ds(start, CHUNK)
        weight = weight_ref[:, at].astype(jnp.float32)
        high, low = split(weight * (1.0 + modulation_ref[1:2, at]))
        scaled_ref[...] += lane_sum(high.astype(jnp.float32) + low.astype(jnp.float32))
        shifted_ref[...] += lane_sum(weight * modulation_ref[0:1, at])
        for first in range(0, tokens, ROWS):
            block = slice(first, min(first + ROWS, tokens))
            total = total_ref[block, :]
            squares = square_ref[block, :]
            for lane in range(0, CHUNK, LANES):
                lanes = pl.ds(pl.multiple_of(start + lane, LANES), LANES)
                part = hidden_ref[block, lanes].astype(jnp.float32)
                total = total + part
                squares = squares + part * part
            total_ref[block, :] = total
            square_ref[block, :] = squares
        return carry + lax.dot_general(
            hidden_ref[:, at],
            jnp.concatenate([high, low], axis=0),
            (((1,), (1,)), ((), ())),
            preferred_element_type=jnp.float32,
        )

    rows = residual_ref.shape[0]
    chunks = width // CHUNK
    early = chunks * 2 // 5
    head = lax.fori_loop(0, early, head_step, jnp.zeros((tokens, 2 * rows), jnp.float32))

    wait_all(got, recv_sems.at[0], members)
    for member, slot, (begin, end), (first, last) in pieces:
        at = (member * slots + slot) * 4
        slotted[at : at + 4, first:last] = got[member, :, begin:end]
    data = slotted[...]
    even = lax.broadcasted_iota(jnp.int32, (span, LANES), 0) % 2 == 0
    nothing = jnp.zeros_like(data)
    spread = jnp.concatenate(
        [jnp.where(even, data, nothing), jnp.where(even, nothing, data)], axis=1
    )
    filtered = dot3((row_high[...], row_low[...]), split(spread), ((1,), (0,)))
    filtered = dot3(split(filtered), (col_high[...], col_low[...]), ((1,), (0,)))
    low_ref[...] = jnp.where(even, filtered[:, :LANES], filtered[:, LANES:])
    for member, slot, (begin, end), (first, last) in pieces:
        at = (member * slots + slot) * 4
        back[member, :, begin:end] = low_ref[at : at + 4, first:last]
    exchange(back, home, send_sems.at[1], recv_sems.at[1], me, members)

    head = lax.fori_loop(early, chunks, head_step, head)
    square = (rows, rows)
    diagonal = lax.broadcasted_iota(jnp.int32, square, 0) == lax.broadcasted_iota(
        jnp.int32, square, 1
    )
    bias = jnp.sum(jnp.where(diagonal, bias_ref[...], 0.0), axis=1, keepdims=True)
    average = jnp.sum(total_ref[...], axis=1, keepdims=True) / D
    second = jnp.sum(square_ref[...], axis=1, keepdims=True) / D
    scale_inv = lax.rsqrt(second - average * average + EPSILON)
    scaled = jnp.sum(scaled_ref[...].T, axis=0, keepdims=True)
    shifted = jnp.sum(shifted_ref[...], axis=1, keepdims=True)
    head = (head[:, :rows] + head[:, rows:] - average * scaled) * scale_inv
    conditional = head.T + (shifted + bias)

    current = step_ref[0]
    last_full = jnp.int32(-1)
    for index in range(NSTEP):
        computed = (skip_ref[index] == 0) & (index <= current)
        last_full = jnp.where(computed, index, last_full)
    spacing = jnp.full((rows, 1), current - last_full, jnp.int32).astype(jnp.float32)
    gap_ratio = spacing / (spacing + 2.0)
    channels = gain_ref.shape[1]
    own = lax.broadcasted_iota(jnp.int32, (rows, channels), 0) // 4 == lax.broadcasted_iota(
        jnp.int32, (rows, channels), 1
    )
    low_gain = jnp.sum(jnp.where(own, gain_ref[0:1, :], 0.0), axis=1, keepdims=True)
    high_gain = jnp.sum(jnp.where(own, gain_ref[1:2, :], 0.0), axis=1, keepdims=True)
    w_low = low_gain * (1.0 + gap_ratio)
    w_high = high_gain * (1.0 - 0.5 * gap_ratio)
    now = jnp.full((rows, 1), current, jnp.int32)
    change = sigma_at(now + 1) - sigma_at(now)

    conditional_ref[...] = conditional
    change_ref[...] = jnp.broadcast_to(change, change_ref.shape)
    wait_all(home, recv_sems.at[1], members)
    for channel in range(members):
        final_ref[4 * channel : 4 * channel + 4, :] = home[channel, :, :tokens]
    low_band = final_ref[...]
    high_band = residual_ref[...] - low_band
    guided_ref[...] = GUIDE_EXTRA * (w_low * low_band + w_high * high_band)
    wait_all(sent, send_sems.at[0], members)
    wait_all(back, send_sems.at[1], members)


def body(
    hidden,
    modulation,
    head_weight,
    head_bias,
    residual,
    latent,
    band_gain,
    cut_rows,
    cut_cols,
    skip_flags,
    step_index,
):
    rows, tokens = residual.shape
    members = PH * PW // tokens
    slots = (tokens + PW - 2) // PW + 1
    owner_each = (
        lax.axis_size("mp") == 1
        and lax.axis_size("seq") == members
        and rows == 4 * members
        and members * slots * 4 == 2 * LANES
        and hidden.shape[1] % CHUNK == 0
    )
    if not owner_each:
        return gathered_body(
            hidden,
            modulation,
            head_weight,
            head_bias,
            residual,
            latent,
            band_gain,
            cut_rows,
            cut_cols,
            skip_flags,
            step_index,
        )
    table = jnp.asarray(filter_tables(members, tokens, slots))
    span = members * slots * 4
    wide = 2 * LANES
    padded = -(-tokens // LANES) * LANES
    block = pltpu.VMEM((members, 4, padded), jnp.float32)
    out = jax.ShapeDtypeStruct((rows, tokens), jnp.float32)
    vmem = pl.BlockSpec(memory_space=pltpu.VMEM)
    operands = (
        hidden,
        head_weight.T,
        table,
        modulation,
        residual,
        head_bias.reshape(1, rows),
        band_gain,
        step_index,
        cut_rows,
        cut_cols,
        skip_flags,
    )
    scalars = 4
    conditional, guided, change = pl.pallas_call(
        functools.partial(step_kernel, members, tokens, slots),
        out_shape=(out, out, out),
        in_specs=[pl.BlockSpec(memory_space=pltpu.HBM)] * len(operands),
        out_specs=(vmem, vmem, vmem),
        scratch_shapes=[pltpu.VMEM(each.shape, each.dtype) for each in operands[:-scalars]]
        + [pltpu.SMEM(each.shape, each.dtype) for each in operands[-scalars:]]
        + [
            block,
            block,
            block,
            block,
            pltpu.VMEM((span, LANES), jnp.float32),
            pltpu.VMEM((span, LANES), jnp.float32),
            pltpu.VMEM((span, span), jnp.bfloat16),
            pltpu.VMEM((span, span), jnp.bfloat16),
            pltpu.VMEM((wide, wide), jnp.bfloat16),
            pltpu.VMEM((wide, wide), jnp.bfloat16),
            pltpu.VMEM((rows, tokens), jnp.float32),
            pltpu.VMEM((tokens, LANES), jnp.float32),
            pltpu.VMEM((tokens, LANES), jnp.float32),
            pltpu.VMEM((rows, LANES), jnp.float32),
            pltpu.VMEM((rows, LANES), jnp.float32),
            pltpu.SemaphoreType.DMA((len(operands) + 3,)),
            pltpu.SemaphoreType.DMA((2,)),
            pltpu.SemaphoreType.DMA((2,)),
        ],
        compiler_params=pltpu.CompilerParams(
            collective_id=0, has_side_effects=True, vmem_limit_bytes=48 * 1024 * 1024
        ),
        cost_estimate=pl.CostEstimate(
            flops=2 * tokens * hidden.shape[1] * rows,
            bytes_accessed=2 * hidden.size + 2 * head_weight.size,
            transcendentals=0,
        ),
    )(*(each if each.size == 1 else pltpu.with_memory_space_constraint(each, pltpu.HBM)
            for each in operands))
    velocity = conditional + guided
    return (velocity, latent + change * velocity)


def solution(mesh):
    in_specs = (
        P(("groups", "seq"), "mp"),
        P("groups", "mp"),
        P("mp", None),
        P("mp"),
        P("mp", ("groups", "seq")),
        P("mp", ("groups", "seq")),
        P(None, "mp"),
        P("groups"),
        P("groups"),
        P("groups"),
        P("groups"),
    )
    out_specs = (P("mp", ("groups", "seq")), P("mp", ("groups", "seq")))
    return jax.shard_map(body, mesh=mesh, in_specs=in_specs, out_specs=out_specs, check_vma=False)
```

```python
import functools
import math

import jax
import jax.numpy as jnp
import ml_dtypes
import numpy as np
from jax import lax
from jax.experimental import pallas as pl
from jax.experimental.pallas import tpu as pltpu
from jax.sharding import PartitionSpec as P

D = 5120
H = 90
W = 160
PH = 45
PW = 80
NSTEP = 50


EPSILON = 1e-06
GUIDE_EXTRA = 4.0
SHIFT_FACTOR = 5.0
HIGHEST = lax.Precision.HIGHEST


def from_partner(value, axis, bit):
    mask = 2**bit
    pairs = [(source, source ^ mask) for source in range(lax.axis_size(axis))]
    return lax.ppermute(value, axis, pairs)


def sigma_at(step_number):
    remain = 1.0 - step_number.astype(jnp.float32) / NSTEP
    return SHIFT_FACTOR * remain / (1.0 + (SHIFT_FACTOR - 1.0) * remain)


def band_weights(skip_flags, step_index, band_gain):
    current = step_index[0]
    counter = jnp.arange(NSTEP, dtype=jnp.int32)
    computed = (skip_flags == 0) & (counter <= current)
    last_full = jnp.max(jnp.where(computed, counter, -1))
    spacing = (current - last_full).astype(jnp.float32)
    gap_ratio = spacing / (spacing + 2.0)
    return (band_gain[0] * (1.0 + gap_ratio), band_gain[1] * (1.0 - 0.5 * gap_ratio))


def band_matrix(length, cutoff):
    counter = jnp.arange(length, dtype=jnp.int32)
    product = counter[:, None] * counter[None, :] % length
    angles = 2.0 * math.pi / length * product.astype(jnp.float32)
    cosine = jnp.cos(angles)
    sine_table = jnp.sin(angles)
    kept_modes = (jnp.minimum(counter, length - counter) <= cutoff).astype(jnp.float32)
    summed = jnp.dot(cosine * kept_modes, cosine.T, precision=HIGHEST) + jnp.dot(
        sine_table * kept_modes, sine_table.T, precision=HIGHEST
    )
    return summed / length


def gathered_body(
    hidden,
    modulation,
    head_weight,
    head_bias,
    residual,
    latent,
    band_gain,
    cut_rows,
    cut_cols,
    skip_flags,
    step_index,
):
    values = hidden.astype(jnp.float32)
    moments = lax.psum((jnp.sum(values, axis=1), jnp.sum(values * values, axis=1)), "mp")
    average = moments[0] / D
    scale_inv = lax.rsqrt(moments[1] / D - average * average + EPSILON)
    normed = (
        (values - average[:, None]) * scale_inv[:, None] * (1.0 + modulation[1]) + modulation[0]
    ).astype(jnp.bfloat16)
    conditional = (
        lax.psum_scatter(
            lax.dot_general(
                head_weight, normed, (((0,), (1,)), ((), ())), preferred_element_type=jnp.float32
            ),
            "mp",
            scatter_dimension=0,
            tiled=True,
        )
        + head_bias[:, None]
    )
    local_rows = residual.shape[0]
    local_tokens = residual.shape[1]
    frame_tokens = PH * PW
    members = frame_tokens // local_tokens
    seq_index = lax.axis_index("seq")
    position = seq_index % members
    frame_index = seq_index // members
    frame_data = residual
    for section_bit in range(members.bit_length() - 1):
        partner = from_partner(frame_data, "seq", section_bit)
        upper_half = seq_index // (1 << section_bit) % 2 == 1
        frame_data = jnp.where(
            upper_half,
            jnp.concatenate([partner, frame_data], axis=1),
            jnp.concatenate([frame_data, partner], axis=1),
        )
    channels = local_rows // 4
    planes = (
        frame_data.reshape(channels, 2, 2, PH, PW).transpose(0, 3, 1, 4, 2).reshape(channels, H, W)
    )
    row_filter = band_matrix(H, cut_rows[frame_index])
    col_filter = band_matrix(W, cut_cols[frame_index])
    row_total = min(local_tokens // PW + 2, PH)
    first_row = jnp.minimum(position * local_tokens // PW, PH - row_total)
    row_part = lax.dynamic_slice_in_dim(row_filter, 2 * first_row, 2 * row_total, 0)
    partial_rows = jnp.einsum("ij,cjw->ciw", row_part, planes, precision=HIGHEST)
    low_rows = jnp.dot(
        partial_rows.reshape(channels * 2 * row_total, W), col_filter, precision=HIGHEST
    ).reshape(channels, 2 * row_total, W)
    low_tokens = (
        low_rows.reshape(channels, row_total, 2, PW, 2)
        .transpose(0, 2, 4, 1, 3)
        .reshape(local_rows, row_total * PW)
    )
    low_band = lax.dynamic_slice_in_dim(
        low_tokens, position * local_tokens - first_row * PW, local_tokens, 1
    )
    high_band = residual - low_band
    w_low, w_high = band_weights(skip_flags, step_index, band_gain)
    row_low = jnp.repeat(w_low, 4)[:, None]
    row_high = jnp.repeat(w_high, 4)[:, None]
    velocity = conditional + GUIDE_EXTRA * (row_low * low_band + row_high * high_band)
    current = step_index[0]
    latent_next = latent + (sigma_at(current + 1) - sigma_at(current)) * velocity
    return (velocity, latent_next)


LANES = 128
CHUNK = 1024
ROWS = 32
MESH = pl.DeviceIdType.MESH


def real_basis(length):
    place = np.arange(length)[:, None]
    column = np.arange(length)[None, :]
    frequency = (column + 1) // 2
    angle = 2.0 * np.pi * (place * frequency % length) / length
    basis = np.where(column % 2 == 1, np.cos(angle), np.sin(angle)) * math.sqrt(2.0 / length)
    basis[:, 0] = 1.0 / math.sqrt(length)
    if length % 2 == 0:
        basis[:, -1] = np.cos(np.pi * np.arange(length)) / math.sqrt(length)
    return basis


def slot_pieces(members, tokens, slots):
    pieces = []
    for member in range(members):
        first = member * tokens // PW
        for slot in range(slots):
            start = max((first + slot) * PW, member * tokens)
            stop = min((first + slot + 1) * PW, (member + 1) * tokens)
            if start < stop:
                pieces.append((
                    member,
                    slot,
                    (start - member * tokens, stop - member * tokens),
                    (start - (first + slot) * PW, stop - (first + slot) * PW),
                ))
    return pieces


def filter_tables(members, tokens, slots):
    rows = np.zeros((members * slots * 4, 2 * LANES))
    row_basis = real_basis(H)
    for member in range(members):
        first = member * tokens // PW
        for slot in range(slots):
            for dy in range(2):
                for dx in range(2):
                    if first + slot < PH:
                        rows[((member * slots + slot) * 2 + dy) * 2 + dx, :H] = row_basis[
                            2 * (first + slot) + dy
                        ]
    cols = np.zeros((2 * LANES, 2 * LANES))
    col_basis = real_basis(W)
    for dx in range(2):
        cols[dx * LANES : dx * LANES + PW, :W] = col_basis[dx::2]
    parts = []
    for table in (rows, cols):
        high = table.astype(np.float32).astype(ml_dtypes.bfloat16)
        low = (table - high.astype(np.float64)).astype(np.float32).astype(ml_dtypes.bfloat16)
        parts += [high, low]
    return np.concatenate(parts, axis=0)


def split(value):
    high = value.astype(jnp.bfloat16)
    return high, (value - high.astype(jnp.float32)).astype(jnp.bfloat16)


def dot3(left, right, dims):
    def one(a, b):
        return lax.dot_general(a, b, (dims, ((), ())), preferred_element_type=jnp.float32)

    return one(left[0], right[0]) + (one(left[0], right[1]) + one(left[1], right[0]))


def far_first(members):
    return sorted(range(1, members), key=lambda step: abs(step - members // 2))


def exchange(source, target, send_sem, recv_sem, me, members):
    for step in far_first(members):
        peer = lax.rem(me + step, members)
        pltpu.make_async_remote_copy(
            src_ref=source.at[peer],
            dst_ref=target.at[me],
            send_sem=send_sem,
            recv_sem=recv_sem,
            device_id={"seq": peer},
            device_id_type=MESH,
        ).start()
    target[me] = source[me]


def wait_all(block_ref, sem, members):
    others = block_ref.at[pl.ds(0, members - 1)]
    pltpu.make_async_copy(others, others, sem).wait()


def step_kernel(
    members,
    tokens,
    slots,
    hidden_hbm,
    weight_hbm,
    table_hbm,
    modulation_hbm,
    residual_hbm,
    bias_hbm,
    gain_hbm,
    step_hbm,
    cut_rows_hbm,
    cut_cols_hbm,
    skip_hbm,
    conditional_ref,
    guided_ref,
    change_ref,
    hidden_ref,
    weight_ref,
    table_ref,
    modulation_ref,
    residual_ref,
    bias_ref,
    gain_ref,
    step_ref,
    cut_rows_ref,
    cut_cols_ref,
    skip_ref,
    sent,
    got,
    back,
    home,
    slotted,
    low_ref,
    row_high,
    row_low,
    col_high,
    col_low,
    final_ref,
    total_ref,
    square_ref,
    load_sems,
    send_sems,
    recv_sems,
):
    me = lax.axis_index("seq")
    width = hidden_ref.shape[1]
    pairs = [
        (residual_hbm, residual_ref),
        (table_hbm, table_ref),
        (cut_rows_hbm, cut_rows_ref),
        (cut_cols_hbm, cut_cols_ref),
        (step_hbm, step_ref),
        (skip_hbm, skip_ref),
    ]
    quarter = width // 4
    for place in range(4):
        part = pl.ds(place * quarter, quarter)
        pairs.append((hidden_hbm.at[:, part], hidden_ref.at[:, part]))
    pairs += [
        (modulation_hbm, modulation_ref),
        (weight_hbm, weight_ref),
        (bias_hbm, bias_ref),
        (gain_hbm, gain_ref),
    ]
    loads = [
        pltpu.make_async_copy(source, target, load_sems.at[place])
        for place, (source, target) in enumerate(pairs)
    ]
    loads[0].start()
    barrier = pltpu.get_barrier_semaphore()
    for step in far_first(members):
        peer = lax.rem(me + step, members)
        pl.semaphore_signal(barrier, inc=1, device_id={"seq": peer}, device_id_type=MESH)
    for load in loads[1:]:
        load.start()
    loads[0].wait()
    for channel in range(members):
        sent[channel, :, :tokens] = residual_ref[4 * channel : 4 * channel + 4, :]
    pl.semaphore_wait(barrier, members - 1)
    exchange(sent, got, send_sems.at[0], recv_sems.at[0], me, members)

    pieces = slot_pieces(members, tokens, slots)
    slotted[...] = jnp.zeros_like(slotted)
    span = members * slots * 4
    wide = 2 * LANES
    for load in loads[1:6]:
        load.wait()
    frequency = (lax.broadcasted_iota(jnp.int32, (1, wide), 1) + 1) // 2
    for base, depth, cut, high_ref, low_part_ref in (
        (0, span, cut_rows_ref[0], row_high, row_low),
        (2 * span, wide, cut_cols_ref[0], col_high, col_low),
    ):
        high = table_ref[base : base + depth, :]
        low = table_ref[base + depth : base + 2 * depth, :]
        kept = (frequency <= cut).astype(jnp.float32).astype(jnp.bfloat16)
        matrix = dot3((high * kept, low * kept), (high, low), ((1,), (1,)))
        high_ref[...], low_part_ref[...] = split(matrix)

    for load in loads[6:10]:
        load.wait()

    def moment_rows(rows):
        total = squares = None
        for lane in range(0, width, LANES):
            part = hidden_ref[rows, lane : lane + LANES].astype(jnp.float32)
            total = part if total is None else total + part
            squares = part * part if squares is None else squares + part * part
        total_ref[rows, :] = total
        square_ref[rows, :] = squares

    def moment_step(index, carry):
        moment_rows(pl.ds(pl.multiple_of(index * ROWS, ROWS), ROWS))
        return carry

    lax.fori_loop(0, tokens // ROWS, moment_step, 0)
    if tokens % ROWS:
        moment_rows(slice(tokens // ROWS * ROWS, tokens))
    average = jnp.sum(total_ref[...], axis=1, keepdims=True) / D
    second = jnp.sum(square_ref[...], axis=1, keepdims=True) / D
    scale_inv = lax.rsqrt(second - average * average + EPSILON)
    total_ref[...] = jnp.broadcast_to(average, total_ref.shape)
    square_ref[...] = jnp.broadcast_to(scale_inv, square_ref.shape)

    for load in loads[10:]:
        load.wait()

    def head_step(index, carry):
        start = pl.multiple_of(index * CHUNK, CHUNK)
        average = total_ref[...]
        scale_inv = square_ref[...]
        parts = []
        for lane in range(0, CHUNK, LANES):
            at = pl.ds(pl.multiple_of(start + lane, LANES), LANES)
            values = hidden_ref[:, at].astype(jnp.float32)
            gain = 1.0 + modulation_ref[1:2, at]
            shift = modulation_ref[0:1, at]
            parts.append(
                ((values - average) * scale_inv * gain + shift).astype(jnp.bfloat16)
            )
        return carry + lax.dot_general(
            jnp.concatenate(parts, axis=1),
            weight_ref[:, pl.ds(start, CHUNK)],
            (((1,), (1,)), ((), ())),
            preferred_element_type=jnp.float32,
        )

    rows = residual_ref.shape[0]
    chunks = width // CHUNK
    early = chunks // 5
    head = lax.fori_loop(0, early, head_step, jnp.zeros((tokens, rows), jnp.float32))

    wait_all(got, recv_sems.at[0], members)
    for member, slot, (begin, end), (first, last) in pieces:
        at = (member * slots + slot) * 4
        slotted[at : at + 4, first:last] = got[member, :, begin:end]
    data = slotted[...]
    even = lax.broadcasted_iota(jnp.int32, (span, LANES), 0) % 2 == 0
    nothing = jnp.zeros_like(data)
    spread = jnp.concatenate(
        [jnp.where(even, data, nothing), jnp.where(even, nothing, data)], axis=1
    )
    filtered = dot3((row_high[...], row_low[...]), split(spread), ((1,), (0,)))
    filtered = dot3(split(filtered), (col_high[...], col_low[...]), ((1,), (0,)))
    low_ref[...] = jnp.where(even, filtered[:, :LANES], filtered[:, LANES:])
    for member, slot, (begin, end), (first, last) in pieces:
        at = (member * slots + slot) * 4
        back[member, :, begin:end] = low_ref[at : at + 4, first:last]
    exchange(back, home, send_sems.at[1], recv_sems.at[1], me, members)

    head = lax.fori_loop(early, chunks, head_step, head)
    square = (rows, rows)
    diagonal = lax.broadcasted_iota(jnp.int32, square, 0) == lax.broadcasted_iota(
        jnp.int32, square, 1
    )
    bias = jnp.sum(jnp.where(diagonal, bias_ref[...], 0.0), axis=1, keepdims=True)
    conditional = head.T + bias

    current = step_ref[0]
    last_full = jnp.int32(-1)
    for index in range(NSTEP):
        computed = (skip_ref[index] == 0) & (index <= current)
        last_full = jnp.where(computed, index, last_full)
    spacing = jnp.full((rows, 1), current - last_full, jnp.int32).astype(jnp.float32)
    gap_ratio = spacing / (spacing + 2.0)
    channels = gain_ref.shape[1]
    own = lax.broadcasted_iota(jnp.int32, (rows, channels), 0) // 4 == lax.broadcasted_iota(
        jnp.int32, (rows, channels), 1
    )
    low_gain = jnp.sum(jnp.where(own, gain_ref[0:1, :], 0.0), axis=1, keepdims=True)
    high_gain = jnp.sum(jnp.where(own, gain_ref[1:2, :], 0.0), axis=1, keepdims=True)
    w_low = low_gain * (1.0 + gap_ratio)
    w_high = high_gain * (1.0 - 0.5 * gap_ratio)
    now = jnp.full((rows, 1), current, jnp.int32)
    change = sigma_at(now + 1) - sigma_at(now)

    conditional_ref[...] = conditional
    change_ref[...] = jnp.broadcast_to(change, change_ref.shape)
    wait_all(home, recv_sems.at[1], members)
    for channel in range(members):
        final_ref[4 * channel : 4 * channel + 4, :] = home[channel, :, :tokens]
    low_band = final_ref[...]
    high_band = residual_ref[...] - low_band
    guided_ref[...] = GUIDE_EXTRA * (w_low * low_band + w_high * high_band)
    wait_all(sent, send_sems.at[0], members)
    wait_all(back, send_sems.at[1], members)


def body(
    hidden,
    modulation,
    head_weight,
    head_bias,
    residual,
    latent,
    band_gain,
    cut_rows,
    cut_cols,
    skip_flags,
    step_index,
):
    rows, tokens = residual.shape
    members = PH * PW // tokens
    slots = (tokens + PW - 2) // PW + 1
    owner_each = (
        lax.axis_size("mp") == 1
        and lax.axis_size("seq") == members
        and rows == 4 * members
        and members * slots * 4 == 2 * LANES
        and hidden.shape[1] % CHUNK == 0
    )
    if not owner_each:
        return gathered_body(
            hidden,
            modulation,
            head_weight,
            head_bias,
            residual,
            latent,
            band_gain,
            cut_rows,
            cut_cols,
            skip_flags,
            step_index,
        )
    table = jnp.asarray(filter_tables(members, tokens, slots))
    span = members * slots * 4
    wide = 2 * LANES
    padded = -(-tokens // LANES) * LANES
    block = pltpu.VMEM((members, 4, padded), jnp.float32)
    out = jax.ShapeDtypeStruct((rows, tokens), jnp.float32)
    vmem = pl.BlockSpec(memory_space=pltpu.VMEM)
    operands = (
        hidden,
        head_weight.T,
        table,
        modulation,
        residual,
        head_bias.reshape(1, rows),
        band_gain,
        step_index,
        cut_rows,
        cut_cols,
        skip_flags,
    )
    scalars = 4
    conditional, guided, change = pl.pallas_call(
        functools.partial(step_kernel, members, tokens, slots),
        out_shape=(out, out, out),
        in_specs=[pl.BlockSpec(memory_space=pltpu.HBM)] * len(operands),
        out_specs=(vmem, vmem, vmem),
        scratch_shapes=[pltpu.VMEM(each.shape, each.dtype) for each in operands[:-scalars]]
        + [pltpu.SMEM(each.shape, each.dtype) for each in operands[-scalars:]]
        + [
            block,
            block,
            block,
            block,
            pltpu.VMEM((span, LANES), jnp.float32),
            pltpu.VMEM((span, LANES), jnp.float32),
            pltpu.VMEM((span, span), jnp.bfloat16),
            pltpu.VMEM((span, span), jnp.bfloat16),
            pltpu.VMEM((wide, wide), jnp.bfloat16),
            pltpu.VMEM((wide, wide), jnp.bfloat16),
            pltpu.VMEM((rows, tokens), jnp.float32),
            pltpu.VMEM((tokens, LANES), jnp.float32),
            pltpu.VMEM((tokens, LANES), jnp.float32),
            pltpu.SemaphoreType.DMA((len(operands) + 3,)),
            pltpu.SemaphoreType.DMA((2,)),
            pltpu.SemaphoreType.DMA((2,)),
        ],
        compiler_params=pltpu.CompilerParams(
            collective_id=0, has_side_effects=True, vmem_limit_bytes=48 * 1024 * 1024
        ),
        cost_estimate=pl.CostEstimate(
            flops=2 * tokens * hidden.shape[1] * rows,
            bytes_accessed=2 * hidden.size + 2 * head_weight.size,
            transcendentals=0,
        ),
    )(*(each if each.size == 1 else pltpu.with_memory_space_constraint(each, pltpu.HBM)
            for each in operands))
    velocity = conditional + guided
    return (velocity, latent + change * velocity)


def solution(mesh):
    in_specs = (
        P(("groups", "seq"), "mp"),
        P("groups", "mp"),
        P("mp", None),
        P("mp"),
        P("mp", ("groups", "seq")),
        P("mp", ("groups", "seq")),
        P(None, "mp"),
        P("groups"),
        P("groups"),
        P("groups"),
        P("groups"),
    )
    out_specs = (P("mp", ("groups", "seq")), P("mp", ("groups", "seq")))
    return jax.shard_map(body, mesh=mesh, in_specs=in_specs, out_specs=out_specs, check_vma=False)
```

```python
import functools
import math

import jax
import jax.numpy as jnp
import ml_dtypes
import numpy as np
from jax import lax
from jax.experimental import pallas as pl
from jax.experimental.pallas import tpu as pltpu
from jax.sharding import PartitionSpec as P

D = 5120
H = 90
W = 160
PH = 45
PW = 80
NSTEP = 50


EPSILON = 1e-06
GUIDE_EXTRA = 4.0
SHIFT_FACTOR = 5.0
HIGHEST = lax.Precision.HIGHEST


def from_partner(value, axis, bit):
    mask = 2**bit
    pairs = [(source, source ^ mask) for source in range(lax.axis_size(axis))]
    return lax.ppermute(value, axis, pairs)


def sigma_at(step_number):
    remain = 1.0 - step_number.astype(jnp.float32) / NSTEP
    return SHIFT_FACTOR * remain / (1.0 + (SHIFT_FACTOR - 1.0) * remain)


def band_weights(skip_flags, step_index, band_gain):
    current = step_index[0]
    counter = jnp.arange(NSTEP, dtype=jnp.int32)
    computed = (skip_flags == 0) & (counter <= current)
    last_full = jnp.max(jnp.where(computed, counter, -1))
    spacing = (current - last_full).astype(jnp.float32)
    gap_ratio = spacing / (spacing + 2.0)
    return (band_gain[0] * (1.0 + gap_ratio), band_gain[1] * (1.0 - 0.5 * gap_ratio))


def band_matrix(length, cutoff):
    counter = jnp.arange(length, dtype=jnp.int32)
    product = counter[:, None] * counter[None, :] % length
    angles = 2.0 * math.pi / length * product.astype(jnp.float32)
    cosine = jnp.cos(angles)
    sine_table = jnp.sin(angles)
    kept_modes = (jnp.minimum(counter, length - counter) <= cutoff).astype(jnp.float32)
    summed = jnp.dot(cosine * kept_modes, cosine.T, precision=HIGHEST) + jnp.dot(
        sine_table * kept_modes, sine_table.T, precision=HIGHEST
    )
    return summed / length


def gathered_body(
    hidden,
    modulation,
    head_weight,
    head_bias,
    residual,
    latent,
    band_gain,
    cut_rows,
    cut_cols,
    skip_flags,
    step_index,
):
    values = hidden.astype(jnp.float32)
    moments = lax.psum((jnp.sum(values, axis=1), jnp.sum(values * values, axis=1)), "mp")
    average = moments[0] / D
    scale_inv = lax.rsqrt(moments[1] / D - average * average + EPSILON)
    normed = (
        (values - average[:, None]) * scale_inv[:, None] * (1.0 + modulation[1]) + modulation[0]
    ).astype(jnp.bfloat16)
    conditional = (
        lax.psum_scatter(
            lax.dot_general(
                head_weight, normed, (((0,), (1,)), ((), ())), preferred_element_type=jnp.float32
            ),
            "mp",
            scatter_dimension=0,
            tiled=True,
        )
        + head_bias[:, None]
    )
    local_rows = residual.shape[0]
    local_tokens = residual.shape[1]
    frame_tokens = PH * PW
    members = frame_tokens // local_tokens
    seq_index = lax.axis_index("seq")
    position = seq_index % members
    frame_index = seq_index // members
    frame_data = residual
    for section_bit in range(members.bit_length() - 1):
        partner = from_partner(frame_data, "seq", section_bit)
        upper_half = seq_index // (1 << section_bit) % 2 == 1
        frame_data = jnp.where(
            upper_half,
            jnp.concatenate([partner, frame_data], axis=1),
            jnp.concatenate([frame_data, partner], axis=1),
        )
    channels = local_rows // 4
    planes = (
        frame_data.reshape(channels, 2, 2, PH, PW).transpose(0, 3, 1, 4, 2).reshape(channels, H, W)
    )
    row_filter = band_matrix(H, cut_rows[frame_index])
    col_filter = band_matrix(W, cut_cols[frame_index])
    row_total = min(local_tokens // PW + 2, PH)
    first_row = jnp.minimum(position * local_tokens // PW, PH - row_total)
    row_part = lax.dynamic_slice_in_dim(row_filter, 2 * first_row, 2 * row_total, 0)
    partial_rows = jnp.einsum("ij,cjw->ciw", row_part, planes, precision=HIGHEST)
    low_rows = jnp.dot(
        partial_rows.reshape(channels * 2 * row_total, W), col_filter, precision=HIGHEST
    ).reshape(channels, 2 * row_total, W)
    low_tokens = (
        low_rows.reshape(channels, row_total, 2, PW, 2)
        .transpose(0, 2, 4, 1, 3)
        .reshape(local_rows, row_total * PW)
    )
    low_band = lax.dynamic_slice_in_dim(
        low_tokens, position * local_tokens - first_row * PW, local_tokens, 1
    )
    high_band = residual - low_band
    w_low, w_high = band_weights(skip_flags, step_index, band_gain)
    row_low = jnp.repeat(w_low, 4)[:, None]
    row_high = jnp.repeat(w_high, 4)[:, None]
    velocity = conditional + GUIDE_EXTRA * (row_low * low_band + row_high * high_band)
    current = step_index[0]
    latent_next = latent + (sigma_at(current + 1) - sigma_at(current)) * velocity
    return (velocity, latent_next)


LANES = 128
CHUNK = 1024
ROWS = 32
MESH = pl.DeviceIdType.MESH


def real_basis(length):
    place = np.arange(length)[:, None]
    column = np.arange(length)[None, :]
    frequency = (column + 1) // 2
    angle = 2.0 * np.pi * (place * frequency % length) / length
    basis = np.where(column % 2 == 1, np.cos(angle), np.sin(angle)) * math.sqrt(2.0 / length)
    basis[:, 0] = 1.0 / math.sqrt(length)
    if length % 2 == 0:
        basis[:, -1] = np.cos(np.pi * np.arange(length)) / math.sqrt(length)
    return basis


def slot_pieces(members, tokens, slots):
    pieces = []
    for member in range(members):
        first = member * tokens // PW
        for slot in range(slots):
            start = max((first + slot) * PW, member * tokens)
            stop = min((first + slot + 1) * PW, (member + 1) * tokens)
            if start < stop:
                pieces.append((
                    member,
                    slot,
                    (start - member * tokens, stop - member * tokens),
                    (start - (first + slot) * PW, stop - (first + slot) * PW),
                ))
    return pieces


def filter_tables(members, tokens, slots):
    rows = np.zeros((members * slots * 4, 2 * LANES))
    row_basis = real_basis(H)
    for member in range(members):
        first = member * tokens // PW
        for slot in range(slots):
            for dy in range(2):
                for dx in range(2):
                    if first + slot < PH:
                        rows[((member * slots + slot) * 2 + dy) * 2 + dx, :H] = row_basis[
                            2 * (first + slot) + dy
                        ]
    cols = np.zeros((2 * LANES, 2 * LANES))
    col_basis = real_basis(W)
    for dx in range(2):
        cols[dx * LANES : dx * LANES + PW, :W] = col_basis[dx::2]
    parts = []
    for table in (rows, cols):
        high = table.astype(np.float32).astype(ml_dtypes.bfloat16)
        low = (table - high.astype(np.float64)).astype(np.float32).astype(ml_dtypes.bfloat16)
        parts += [high, low]
    return np.concatenate(parts, axis=0)


def split(value):
    high = value.astype(jnp.bfloat16)
    return high, (value - high.astype(jnp.float32)).astype(jnp.bfloat16)


def dot3(left, right, dims):
    def one(a, b):
        return lax.dot_general(a, b, (dims, ((), ())), preferred_element_type=jnp.float32)

    return one(left[0], right[0]) + (one(left[0], right[1]) + one(left[1], right[0]))


def far_first(members):
    return sorted(range(1, members), key=lambda step: abs(step - members // 2))


def exchange(source, target, send_sem, recv_sem, me, members):
    for step in far_first(members):
        peer = lax.rem(me + step, members)
        pltpu.make_async_remote_copy(
            src_ref=source.at[peer],
            dst_ref=target.at[me],
            send_sem=send_sem,
            recv_sem=recv_sem,
            device_id={"seq": peer},
            device_id_type=MESH,
        ).start()
    target[me] = source[me]


def wait_all(block_ref, sem, members):
    others = block_ref.at[pl.ds(0, members - 1)]
    pltpu.make_async_copy(others, others, sem).wait()


def step_kernel(
    members,
    tokens,
    slots,
    hidden_hbm,
    weight_hbm,
    table_hbm,
    modulation_hbm,
    residual_hbm,
    bias_hbm,
    gain_hbm,
    step_hbm,
    cut_rows_hbm,
    cut_cols_hbm,
    skip_hbm,
    conditional_ref,
    guided_ref,
    change_ref,
    hidden_ref,
    weight_ref,
    table_ref,
    modulation_ref,
    residual_ref,
    bias_ref,
    gain_ref,
    step_ref,
    cut_rows_ref,
    cut_cols_ref,
    skip_ref,
    sent,
    got,
    back,
    home,
    slotted,
    low_ref,
    row_high,
    row_low,
    col_high,
    col_low,
    final_ref,
    total_ref,
    square_ref,
    load_sems,
    send_sems,
    recv_sems,
):
    me = lax.axis_index("seq")
    width = hidden_ref.shape[1]
    pairs = [
        (residual_hbm, residual_ref),
        (table_hbm, table_ref),
        (cut_rows_hbm, cut_rows_ref),
        (cut_cols_hbm, cut_cols_ref),
        (step_hbm, step_ref),
        (skip_hbm, skip_ref),
    ]
    quarter = width // 4
    for place in range(4):
        part = pl.ds(place * quarter, quarter)
        pairs.append((hidden_hbm.at[:, part], hidden_ref.at[:, part]))
    pairs += [
        (modulation_hbm, modulation_ref),
        (weight_hbm, weight_ref),
        (bias_hbm, bias_ref),
        (gain_hbm, gain_ref),
    ]
    loads = [
        pltpu.make_async_copy(source, target, load_sems.at[place])
        for place, (source, target) in enumerate(pairs)
    ]
    loads[0].start()
    barrier = pltpu.get_barrier_semaphore()
    for step in far_first(members):
        peer = lax.rem(me + step, members)
        pl.semaphore_signal(barrier, inc=1, device_id={"seq": peer}, device_id_type=MESH)
    for load in loads[1:]:
        load.start()
    loads[0].wait()
    for channel in range(members):
        sent[channel, :, :tokens] = residual_ref[4 * channel : 4 * channel + 4, :]
    pl.semaphore_wait(barrier, members - 1)
    exchange(sent, got, send_sems.at[0], recv_sems.at[0], me, members)

    pieces = slot_pieces(members, tokens, slots)
    slotted[...] = jnp.zeros_like(slotted)
    span = members * slots * 4
    wide = 2 * LANES
    for load in loads[1:6]:
        load.wait()
    frequency = (lax.broadcasted_iota(jnp.int32, (1, wide), 1) + 1) // 2
    for base, depth, cut, high_ref, low_part_ref in (
        (0, span, cut_rows_ref[0], row_high, row_low),
        (2 * span, wide, cut_cols_ref[0], col_high, col_low),
    ):
        high = table_ref[base : base + depth, :]
        low = table_ref[base + depth : base + 2 * depth, :]
        kept = (frequency <= cut).astype(jnp.float32).astype(jnp.bfloat16)
        matrix = dot3((high * kept, low * kept), (high, low), ((1,), (1,)))
        high_ref[...], low_part_ref[...] = split(matrix)

    for load in loads[6:10]:
        load.wait()

    def moment_rows(rows):
        total = squares = None
        for lane in range(0, width, LANES):
            part = hidden_ref[rows, lane : lane + LANES].astype(jnp.float32)
            total = part if total is None else total + part
            squares = part * part if squares is None else squares + part * part
        total_ref[rows, :] = total
        square_ref[rows, :] = squares

    def moment_step(index, carry):
        moment_rows(pl.ds(pl.multiple_of(index * ROWS, ROWS), ROWS))
        return carry

    lax.fori_loop(0, tokens // ROWS, moment_step, 0)
    if tokens % ROWS:
        moment_rows(slice(tokens // ROWS * ROWS, tokens))
    average = jnp.sum(total_ref[...], axis=1, keepdims=True) / D
    second = jnp.sum(square_ref[...], axis=1, keepdims=True) / D
    scale_inv = lax.rsqrt(second - average * average + EPSILON)
    total_ref[...] = jnp.broadcast_to(average, total_ref.shape)
    square_ref[...] = jnp.broadcast_to(scale_inv, square_ref.shape)

    for load in loads[10:]:
        load.wait()

    def head_step(index, carry):
        start = pl.multiple_of(index * CHUNK, CHUNK)
        average = total_ref[...]
        scale_inv = square_ref[...]
        parts = []
        for lane in range(0, CHUNK, LANES):
            at = pl.ds(pl.multiple_of(start + lane, LANES), LANES)
            values = hidden_ref[:, at].astype(jnp.float32)
            gain = 1.0 + modulation_ref[1:2, at]
            shift = modulation_ref[0:1, at]
            parts.append(
                ((values - average) * scale_inv * gain + shift).astype(jnp.bfloat16)
            )
        return carry + lax.dot_general(
            jnp.concatenate(parts, axis=1),
            weight_ref[:, pl.ds(start, CHUNK)],
            (((1,), (1,)), ((), ())),
            preferred_element_type=jnp.float32,
        )

    rows = residual_ref.shape[0]
    chunks = width // CHUNK
    early = chunks * 3 // 5
    head = lax.fori_loop(0, early, head_step, jnp.zeros((tokens, rows), jnp.float32))

    wait_all(got, recv_sems.at[0], members)
    for member, slot, (begin, end), (first, last) in pieces:
        at = (member * slots + slot) * 4
        slotted[at : at + 4, first:last] = got[member, :, begin:end]
    data = slotted[...]
    even = lax.broadcasted_iota(jnp.int32, (span, LANES), 0) % 2 == 0
    nothing = jnp.zeros_like(data)
    spread = jnp.concatenate(
        [jnp.where(even, data, nothing), jnp.where(even, nothing, data)], axis=1
    )
    filtered = dot3((row_high[...], row_low[...]), split(spread), ((1,), (0,)))
    filtered = dot3(split(filtered), (col_high[...], col_low[...]), ((1,), (0,)))
    low_ref[...] = jnp.where(even, filtered[:, :LANES], filtered[:, LANES:])
    for member, slot, (begin, end), (first, last) in pieces:
        at = (member * slots + slot) * 4
        back[member, :, begin:end] = low_ref[at : at + 4, first:last]
    exchange(back, home, send_sems.at[1], recv_sems.at[1], me, members)

    head = lax.fori_loop(early, chunks, head_step, head)
    square = (rows, rows)
    diagonal = lax.broadcasted_iota(jnp.int32, square, 0) == lax.broadcasted_iota(
        jnp.int32, square, 1
    )
    bias = jnp.sum(jnp.where(diagonal, bias_ref[...], 0.0), axis=1, keepdims=True)
    conditional = head.T + bias

    current = step_ref[0]
    last_full = jnp.int32(-1)
    for index in range(NSTEP):
        computed = (skip_ref[index] == 0) & (index <= current)
        last_full = jnp.where(computed, index, last_full)
    spacing = jnp.full((rows, 1), current - last_full, jnp.int32).astype(jnp.float32)
    gap_ratio = spacing / (spacing + 2.0)
    channels = gain_ref.shape[1]
    own = lax.broadcasted_iota(jnp.int32, (rows, channels), 0) // 4 == lax.broadcasted_iota(
        jnp.int32, (rows, channels), 1
    )
    low_gain = jnp.sum(jnp.where(own, gain_ref[0:1, :], 0.0), axis=1, keepdims=True)
    high_gain = jnp.sum(jnp.where(own, gain_ref[1:2, :], 0.0), axis=1, keepdims=True)
    w_low = low_gain * (1.0 + gap_ratio)
    w_high = high_gain * (1.0 - 0.5 * gap_ratio)
    now = jnp.full((rows, 1), current, jnp.int32)
    change = sigma_at(now + 1) - sigma_at(now)

    conditional_ref[...] = conditional
    change_ref[...] = jnp.broadcast_to(change, change_ref.shape)
    wait_all(home, recv_sems.at[1], members)
    for channel in range(members):
        final_ref[4 * channel : 4 * channel + 4, :] = home[channel, :, :tokens]
    low_band = final_ref[...]
    high_band = residual_ref[...] - low_band
    guided_ref[...] = GUIDE_EXTRA * (w_low * low_band + w_high * high_band)
    wait_all(sent, send_sems.at[0], members)
    wait_all(back, send_sems.at[1], members)


def body(
    hidden,
    modulation,
    head_weight,
    head_bias,
    residual,
    latent,
    band_gain,
    cut_rows,
    cut_cols,
    skip_flags,
    step_index,
):
    rows, tokens = residual.shape
    members = PH * PW // tokens
    slots = (tokens + PW - 2) // PW + 1
    owner_each = (
        lax.axis_size("mp") == 1
        and lax.axis_size("seq") == members
        and rows == 4 * members
        and members * slots * 4 == 2 * LANES
        and hidden.shape[1] % CHUNK == 0
    )
    if not owner_each:
        return gathered_body(
            hidden,
            modulation,
            head_weight,
            head_bias,
            residual,
            latent,
            band_gain,
            cut_rows,
            cut_cols,
            skip_flags,
            step_index,
        )
    table = jnp.asarray(filter_tables(members, tokens, slots))
    span = members * slots * 4
    wide = 2 * LANES
    padded = -(-tokens // LANES) * LANES
    block = pltpu.VMEM((members, 4, padded), jnp.float32)
    out = jax.ShapeDtypeStruct((rows, tokens), jnp.float32)
    vmem = pl.BlockSpec(memory_space=pltpu.VMEM)
    operands = (
        hidden,
        head_weight.T,
        table,
        modulation,
        residual,
        head_bias.reshape(1, rows),
        band_gain,
        step_index,
        cut_rows,
        cut_cols,
        skip_flags,
    )
    scalars = 4
    conditional, guided, change = pl.pallas_call(
        functools.partial(step_kernel, members, tokens, slots),
        out_shape=(out, out, out),
        in_specs=[pl.BlockSpec(memory_space=pltpu.HBM)] * len(operands),
        out_specs=(vmem, vmem, vmem),
        scratch_shapes=[pltpu.VMEM(each.shape, each.dtype) for each in operands[:-scalars]]
        + [pltpu.SMEM(each.shape, each.dtype) for each in operands[-scalars:]]
        + [
            block,
            block,
            block,
            block,
            pltpu.VMEM((span, LANES), jnp.float32),
            pltpu.VMEM((span, LANES), jnp.float32),
            pltpu.VMEM((span, span), jnp.bfloat16),
            pltpu.VMEM((span, span), jnp.bfloat16),
            pltpu.VMEM((wide, wide), jnp.bfloat16),
            pltpu.VMEM((wide, wide), jnp.bfloat16),
            pltpu.VMEM((rows, tokens), jnp.float32),
            pltpu.VMEM((tokens, LANES), jnp.float32),
            pltpu.VMEM((tokens, LANES), jnp.float32),
            pltpu.SemaphoreType.DMA((len(operands) + 3,)),
            pltpu.SemaphoreType.DMA((2,)),
            pltpu.SemaphoreType.DMA((2,)),
        ],
        compiler_params=pltpu.CompilerParams(
            collective_id=0, has_side_effects=True, vmem_limit_bytes=48 * 1024 * 1024
        ),
        cost_estimate=pl.CostEstimate(
            flops=2 * tokens * hidden.shape[1] * rows,
            bytes_accessed=2 * hidden.size + 2 * head_weight.size,
            transcendentals=0,
        ),
    )(*(each if each.size == 1 else pltpu.with_memory_space_constraint(each, pltpu.HBM)
            for each in operands))
    velocity = conditional + guided
    return (velocity, latent + change * velocity)


def solution(mesh):
    in_specs = (
        P(("groups", "seq"), "mp"),
        P("groups", "mp"),
        P("mp", None),
        P("mp"),
        P("mp", ("groups", "seq")),
        P("mp", ("groups", "seq")),
        P(None, "mp"),
        P("groups"),
        P("groups"),
        P("groups"),
        P("groups"),
    )
    out_specs = (P("mp", ("groups", "seq")), P("mp", ("groups", "seq")))
    return jax.shard_map(body, mesh=mesh, in_specs=in_specs, out_specs=out_specs, check_vma=False)
```

```python
import functools
import math

import jax
import jax.numpy as jnp
import ml_dtypes
import numpy as np
from jax import lax
from jax.experimental import pallas as pl
from jax.experimental.pallas import tpu as pltpu
from jax.sharding import PartitionSpec as P

D = 5120
H = 90
W = 160
PH = 45
PW = 80
NSTEP = 50


EPSILON = 1e-06
GUIDE_EXTRA = 4.0
SHIFT_FACTOR = 5.0
HIGHEST = lax.Precision.HIGHEST


def from_partner(value, axis, bit):
    mask = 2**bit
    pairs = [(source, source ^ mask) for source in range(lax.axis_size(axis))]
    return lax.ppermute(value, axis, pairs)


def sigma_at(step_number):
    remain = 1.0 - step_number.astype(jnp.float32) / NSTEP
    return SHIFT_FACTOR * remain / (1.0 + (SHIFT_FACTOR - 1.0) * remain)


def band_weights(skip_flags, step_index, band_gain):
    current = step_index[0]
    counter = jnp.arange(NSTEP, dtype=jnp.int32)
    computed = (skip_flags == 0) & (counter <= current)
    last_full = jnp.max(jnp.where(computed, counter, -1))
    spacing = (current - last_full).astype(jnp.float32)
    gap_ratio = spacing / (spacing + 2.0)
    return (band_gain[0] * (1.0 + gap_ratio), band_gain[1] * (1.0 - 0.5 * gap_ratio))


def band_matrix(length, cutoff):
    counter = jnp.arange(length, dtype=jnp.int32)
    product = counter[:, None] * counter[None, :] % length
    angles = 2.0 * math.pi / length * product.astype(jnp.float32)
    cosine = jnp.cos(angles)
    sine_table = jnp.sin(angles)
    kept_modes = (jnp.minimum(counter, length - counter) <= cutoff).astype(jnp.float32)
    summed = jnp.dot(cosine * kept_modes, cosine.T, precision=HIGHEST) + jnp.dot(
        sine_table * kept_modes, sine_table.T, precision=HIGHEST
    )
    return summed / length


def gathered_body(
    hidden,
    modulation,
    head_weight,
    head_bias,
    residual,
    latent,
    band_gain,
    cut_rows,
    cut_cols,
    skip_flags,
    step_index,
):
    values = hidden.astype(jnp.float32)
    moments = lax.psum((jnp.sum(values, axis=1), jnp.sum(values * values, axis=1)), "mp")
    average = moments[0] / D
    scale_inv = lax.rsqrt(moments[1] / D - average * average + EPSILON)
    normed = (
        (values - average[:, None]) * scale_inv[:, None] * (1.0 + modulation[1]) + modulation[0]
    ).astype(jnp.bfloat16)
    conditional = (
        lax.psum_scatter(
            lax.dot_general(
                head_weight, normed, (((0,), (1,)), ((), ())), preferred_element_type=jnp.float32
            ),
            "mp",
            scatter_dimension=0,
            tiled=True,
        )
        + head_bias[:, None]
    )
    local_rows = residual.shape[0]
    local_tokens = residual.shape[1]
    frame_tokens = PH * PW
    members = frame_tokens // local_tokens
    seq_index = lax.axis_index("seq")
    position = seq_index % members
    frame_index = seq_index // members
    frame_data = residual
    for section_bit in range(members.bit_length() - 1):
        partner = from_partner(frame_data, "seq", section_bit)
        upper_half = seq_index // (1 << section_bit) % 2 == 1
        frame_data = jnp.where(
            upper_half,
            jnp.concatenate([partner, frame_data], axis=1),
            jnp.concatenate([frame_data, partner], axis=1),
        )
    channels = local_rows // 4
    planes = (
        frame_data.reshape(channels, 2, 2, PH, PW).transpose(0, 3, 1, 4, 2).reshape(channels, H, W)
    )
    row_filter = band_matrix(H, cut_rows[frame_index])
    col_filter = band_matrix(W, cut_cols[frame_index])
    row_total = min(local_tokens // PW + 2, PH)
    first_row = jnp.minimum(position * local_tokens // PW, PH - row_total)
    row_part = lax.dynamic_slice_in_dim(row_filter, 2 * first_row, 2 * row_total, 0)
    partial_rows = jnp.einsum("ij,cjw->ciw", row_part, planes, precision=HIGHEST)
    low_rows = jnp.dot(
        partial_rows.reshape(channels * 2 * row_total, W), col_filter, precision=HIGHEST
    ).reshape(channels, 2 * row_total, W)
    low_tokens = (
        low_rows.reshape(channels, row_total, 2, PW, 2)
        .transpose(0, 2, 4, 1, 3)
        .reshape(local_rows, row_total * PW)
    )
    low_band = lax.dynamic_slice_in_dim(
        low_tokens, position * local_tokens - first_row * PW, local_tokens, 1
    )
    high_band = residual - low_band
    w_low, w_high = band_weights(skip_flags, step_index, band_gain)
    row_low = jnp.repeat(w_low, 4)[:, None]
    row_high = jnp.repeat(w_high, 4)[:, None]
    velocity = conditional + GUIDE_EXTRA * (row_low * low_band + row_high * high_band)
    current = step_index[0]
    latent_next = latent + (sigma_at(current + 1) - sigma_at(current)) * velocity
    return (velocity, latent_next)


LANES = 128
CHUNK = 1024
ROWS = 32
MESH = pl.DeviceIdType.MESH


def real_basis(length):
    place = np.arange(length)[:, None]
    column = np.arange(length)[None, :]
    frequency = (column + 1) // 2
    angle = 2.0 * np.pi * (place * frequency % length) / length
    basis = np.where(column % 2 == 1, np.cos(angle), np.sin(angle)) * math.sqrt(2.0 / length)
    basis[:, 0] = 1.0 / math.sqrt(length)
    if length % 2 == 0:
        basis[:, -1] = np.cos(np.pi * np.arange(length)) / math.sqrt(length)
    return basis


def slot_pieces(members, tokens, slots):
    pieces = []
    for member in range(members):
        first = member * tokens // PW
        for slot in range(slots):
            start = max((first + slot) * PW, member * tokens)
            stop = min((first + slot + 1) * PW, (member + 1) * tokens)
            if start < stop:
                pieces.append((
                    member,
                    slot,
                    (start - member * tokens, stop - member * tokens),
                    (start - (first + slot) * PW, stop - (first + slot) * PW),
                ))
    return pieces


def filter_tables(members, tokens, slots):
    rows = np.zeros((members * slots * 4, 2 * LANES))
    row_basis = real_basis(H)
    for member in range(members):
        first = member * tokens // PW
        for slot in range(slots):
            for dy in range(2):
                for dx in range(2):
                    if first + slot < PH:
                        rows[((member * slots + slot) * 2 + dy) * 2 + dx, :H] = row_basis[
                            2 * (first + slot) + dy
                        ]
    cols = np.zeros((2 * LANES, 2 * LANES))
    col_basis = real_basis(W)
    for dx in range(2):
        cols[dx * LANES : dx * LANES + PW, :W] = col_basis[dx::2]
    parts = []
    for table in (rows, cols):
        high = table.astype(np.float32).astype(ml_dtypes.bfloat16)
        low = (table - high.astype(np.float64)).astype(np.float32).astype(ml_dtypes.bfloat16)
        parts += [high, low]
    return np.concatenate(parts, axis=0)


def split(value):
    high = value.astype(jnp.bfloat16)
    return high, (value - high.astype(jnp.float32)).astype(jnp.bfloat16)


def dot3(left, right, dims):
    def one(a, b):
        return lax.dot_general(a, b, (dims, ((), ())), preferred_element_type=jnp.float32)

    return one(left[0], right[0]) + (one(left[0], right[1]) + one(left[1], right[0]))


def far_first(members):
    return range(1, members)


def exchange(source, target, send_sem, recv_sem, me, members):
    for step in far_first(members):
        peer = lax.rem(me + step, members)
        pltpu.make_async_remote_copy(
            src_ref=source.at[peer],
            dst_ref=target.at[me],
            send_sem=send_sem,
            recv_sem=recv_sem,
            device_id={"seq": peer},
            device_id_type=MESH,
        ).start()
    target[me] = source[me]


def wait_all(block_ref, sem, members):
    others = block_ref.at[pl.ds(0, members - 1)]
    pltpu.make_async_copy(others, others, sem).wait()


def step_kernel(
    members,
    tokens,
    slots,
    hidden_hbm,
    weight_hbm,
    table_hbm,
    modulation_hbm,
    residual_hbm,
    bias_hbm,
    gain_hbm,
    step_hbm,
    cut_rows_hbm,
    cut_cols_hbm,
    skip_hbm,
    conditional_ref,
    guided_ref,
    change_ref,
    hidden_ref,
    weight_ref,
    table_ref,
    modulation_ref,
    residual_ref,
    bias_ref,
    gain_ref,
    step_ref,
    cut_rows_ref,
    cut_cols_ref,
    skip_ref,
    sent,
    got,
    back,
    home,
    slotted,
    low_ref,
    row_high,
    row_low,
    col_high,
    col_low,
    final_ref,
    total_ref,
    square_ref,
    load_sems,
    send_sems,
    recv_sems,
):
    me = lax.axis_index("seq")
    width = hidden_ref.shape[1]
    pairs = [
        (residual_hbm, residual_ref),
        (table_hbm, table_ref),
        (cut_rows_hbm, cut_rows_ref),
        (cut_cols_hbm, cut_cols_ref),
        (step_hbm, step_ref),
        (skip_hbm, skip_ref),
    ]
    quarter = width // 4
    for place in range(4):
        part = pl.ds(place * quarter, quarter)
        pairs.append((hidden_hbm.at[:, part], hidden_ref.at[:, part]))
    pairs += [
        (modulation_hbm, modulation_ref),
        (weight_hbm, weight_ref),
        (bias_hbm, bias_ref),
        (gain_hbm, gain_ref),
    ]
    loads = [
        pltpu.make_async_copy(source, target, load_sems.at[place])
        for place, (source, target) in enumerate(pairs)
    ]
    loads[0].start()
    barrier = pltpu.get_barrier_semaphore()
    for step in far_first(members):
        peer = lax.rem(me + step, members)
        pl.semaphore_signal(barrier, inc=1, device_id={"seq": peer}, device_id_type=MESH)
    for load in loads[1:]:
        load.start()
    loads[0].wait()
    for channel in range(members):
        sent[channel, :, :tokens] = residual_ref[4 * channel : 4 * channel + 4, :]
    pl.semaphore_wait(barrier, members - 1)
    exchange(sent, got, send_sems.at[0], recv_sems.at[0], me, members)

    pieces = slot_pieces(members, tokens, slots)
    slotted[...] = jnp.zeros_like(slotted)
    span = members * slots * 4
    wide = 2 * LANES
    for load in loads[1:6]:
        load.wait()
    frequency = (lax.broadcasted_iota(jnp.int32, (1, wide), 1) + 1) // 2
    for base, depth, cut, high_ref, low_part_ref in (
        (0, span, cut_rows_ref[0], row_high, row_low),
        (2 * span, wide, cut_cols_ref[0], col_high, col_low),
    ):
        high = table_ref[base : base + depth, :]
        low = table_ref[base + depth : base + 2 * depth, :]
        kept = (frequency <= cut).astype(jnp.float32).astype(jnp.bfloat16)
        matrix = dot3((high * kept, low * kept), (high, low), ((1,), (1,)))
        high_ref[...], low_part_ref[...] = split(matrix)

    for load in loads[6:10]:
        load.wait()

    def moment_rows(rows):
        total = squares = None
        for lane in range(0, width, LANES):
            part = hidden_ref[rows, lane : lane + LANES].astype(jnp.float32)
            total = part if total is None else total + part
            squares = part * part if squares is None else squares + part * part
        total_ref[rows, :] = total
        square_ref[rows, :] = squares

    def moment_step(index, carry):
        moment_rows(pl.ds(pl.multiple_of(index * ROWS, ROWS), ROWS))
        return carry

    lax.fori_loop(0, tokens // ROWS, moment_step, 0)
    if tokens % ROWS:
        moment_rows(slice(tokens // ROWS * ROWS, tokens))
    average = jnp.sum(total_ref[...], axis=1, keepdims=True) / D
    second = jnp.sum(square_ref[...], axis=1, keepdims=True) / D
    scale_inv = lax.rsqrt(second - average * average + EPSILON)
    total_ref[...] = jnp.broadcast_to(average, total_ref.shape)
    square_ref[...] = jnp.broadcast_to(scale_inv, square_ref.shape)

    for load in loads[10:]:
        load.wait()

    def head_step(index, carry):
        start = pl.multiple_of(index * CHUNK, CHUNK)
        average = total_ref[...]
        scale_inv = square_ref[...]
        parts = []
        for lane in range(0, CHUNK, LANES):
            at = pl.ds(pl.multiple_of(start + lane, LANES), LANES)
            values = hidden_ref[:, at].astype(jnp.float32)
            gain = 1.0 + modulation_ref[1:2, at]
            shift = modulation_ref[0:1, at]
            parts.append(
                ((values - average) * scale_inv * gain + shift).astype(jnp.bfloat16)
            )
        return carry + lax.dot_general(
            jnp.concatenate(parts, axis=1),
            weight_ref[:, pl.ds(start, CHUNK)],
            (((1,), (1,)), ((), ())),
            preferred_element_type=jnp.float32,
        )

    rows = residual_ref.shape[0]
    chunks = width // CHUNK
    early = chunks * 3 // 5
    head = lax.fori_loop(0, early, head_step, jnp.zeros((tokens, rows), jnp.float32))

    wait_all(got, recv_sems.at[0], members)
    for member, slot, (begin, end), (first, last) in pieces:
        at = (member * slots + slot) * 4
        slotted[at : at + 4, first:last] = got[member, :, begin:end]
    data = slotted[...]
    even = lax.broadcasted_iota(jnp.int32, (span, LANES), 0) % 2 == 0
    nothing = jnp.zeros_like(data)
    spread = jnp.concatenate(
        [jnp.where(even, data, nothing), jnp.where(even, nothing, data)], axis=1
    )
    spread = split(spread)
    half = span // 2
    for base in (0, half):
        rows_at = slice(base, base + half)
        filtered = dot3((row_high[rows_at, :], row_low[rows_at, :]), spread, ((1,), (0,)))
        filtered = dot3(split(filtered), (col_high[...], col_low[...]), ((1,), (0,)))
        low_ref[rows_at, :] = jnp.where(
            even[rows_at, :], filtered[:, :LANES], filtered[:, LANES:]
        )
        for member, slot, (begin, end), (first, last) in pieces:
            at = (member * slots + slot) * 4
            if base <= at < base + half:
                back[member, :, begin:end] = low_ref[at : at + 4, first:last]
        for member in range(base // (4 * slots), (base + half) // (4 * slots)):

            @pl.when(me != member)
            def _(member=member):
                pltpu.make_async_remote_copy(
                    src_ref=back.at[member],
                    dst_ref=home.at[me],
                    send_sem=send_sems.at[1],
                    recv_sem=recv_sems.at[1],
                    device_id={"seq": member},
                    device_id_type=MESH,
                ).start()

    home[me] = back[me]
    head = lax.fori_loop(early, chunks, head_step, head)
    square = (rows, rows)
    diagonal = lax.broadcasted_iota(jnp.int32, square, 0) == lax.broadcasted_iota(
        jnp.int32, square, 1
    )
    bias = jnp.sum(jnp.where(diagonal, bias_ref[...], 0.0), axis=1, keepdims=True)
    conditional = head.T + bias

    current = step_ref[0]
    last_full = jnp.int32(-1)
    for index in range(NSTEP):
        computed = (skip_ref[index] == 0) & (index <= current)
        last_full = jnp.where(computed, index, last_full)
    spacing = jnp.full((rows, 1), current - last_full, jnp.int32).astype(jnp.float32)
    gap_ratio = spacing / (spacing + 2.0)
    channels = gain_ref.shape[1]
    own = lax.broadcasted_iota(jnp.int32, (rows, channels), 0) // 4 == lax.broadcasted_iota(
        jnp.int32, (rows, channels), 1
    )
    low_gain = jnp.sum(jnp.where(own, gain_ref[0:1, :], 0.0), axis=1, keepdims=True)
    high_gain = jnp.sum(jnp.where(own, gain_ref[1:2, :], 0.0), axis=1, keepdims=True)
    w_low = low_gain * (1.0 + gap_ratio)
    w_high = high_gain * (1.0 - 0.5 * gap_ratio)
    now = jnp.full((rows, 1), current, jnp.int32)
    change = sigma_at(now + 1) - sigma_at(now)

    conditional_ref[...] = conditional
    change_ref[...] = jnp.broadcast_to(change, change_ref.shape)
    wait_all(home, recv_sems.at[1], members)
    for channel in range(members):
        final_ref[4 * channel : 4 * channel + 4, :] = home[channel, :, :tokens]
    low_band = final_ref[...]
    high_band = residual_ref[...] - low_band
    guided_ref[...] = GUIDE_EXTRA * (w_low * low_band + w_high * high_band)
    wait_all(sent, send_sems.at[0], members)
    wait_all(back, send_sems.at[1], members)


def body(
    hidden,
    modulation,
    head_weight,
    head_bias,
    residual,
    latent,
    band_gain,
    cut_rows,
    cut_cols,
    skip_flags,
    step_index,
):
    rows, tokens = residual.shape
    members = PH * PW // tokens
    slots = (tokens + PW - 2) // PW + 1
    owner_each = (
        lax.axis_size("mp") == 1
        and lax.axis_size("seq") == members
        and rows == 4 * members
        and members * slots * 4 == 2 * LANES
        and hidden.shape[1] % CHUNK == 0
    )
    if not owner_each:
        return gathered_body(
            hidden,
            modulation,
            head_weight,
            head_bias,
            residual,
            latent,
            band_gain,
            cut_rows,
            cut_cols,
            skip_flags,
            step_index,
        )
    table = jnp.asarray(filter_tables(members, tokens, slots))
    span = members * slots * 4
    wide = 2 * LANES
    padded = -(-tokens // LANES) * LANES
    block = pltpu.VMEM((members, 4, padded), jnp.float32)
    out = jax.ShapeDtypeStruct((rows, tokens), jnp.float32)
    vmem = pl.BlockSpec(memory_space=pltpu.VMEM)
    operands = (
        hidden,
        head_weight.T,
        table,
        modulation,
        residual,
        head_bias.reshape(1, rows),
        band_gain,
        step_index,
        cut_rows,
        cut_cols,
        skip_flags,
    )
    scalars = 4
    conditional, guided, change = pl.pallas_call(
        functools.partial(step_kernel, members, tokens, slots),
        out_shape=(out, out, out),
        in_specs=[pl.BlockSpec(memory_space=pltpu.HBM)] * len(operands),
        out_specs=(vmem, vmem, vmem),
        scratch_shapes=[pltpu.VMEM(each.shape, each.dtype) for each in operands[:-scalars]]
        + [pltpu.SMEM(each.shape, each.dtype) for each in operands[-scalars:]]
        + [
            block,
            block,
            block,
            block,
            pltpu.VMEM((span, LANES), jnp.float32),
            pltpu.VMEM((span, LANES), jnp.float32),
            pltpu.VMEM((span, span), jnp.bfloat16),
            pltpu.VMEM((span, span), jnp.bfloat16),
            pltpu.VMEM((wide, wide), jnp.bfloat16),
            pltpu.VMEM((wide, wide), jnp.bfloat16),
            pltpu.VMEM((rows, tokens), jnp.float32),
            pltpu.VMEM((tokens, LANES), jnp.float32),
            pltpu.VMEM((tokens, LANES), jnp.float32),
            pltpu.SemaphoreType.DMA((len(operands) + 3,)),
            pltpu.SemaphoreType.DMA((2,)),
            pltpu.SemaphoreType.DMA((2,)),
        ],
        compiler_params=pltpu.CompilerParams(
            collective_id=0, has_side_effects=True, vmem_limit_bytes=48 * 1024 * 1024
        ),
        cost_estimate=pl.CostEstimate(
            flops=2 * tokens * hidden.shape[1] * rows,
            bytes_accessed=2 * hidden.size + 2 * head_weight.size,
            transcendentals=0,
        ),
    )(*(each if each.size == 1 else pltpu.with_memory_space_constraint(each, pltpu.HBM)
            for each in operands))
    velocity = conditional + guided
    return (velocity, latent + change * velocity)


def solution(mesh):
    in_specs = (
        P(("groups", "seq"), "mp"),
        P("groups", "mp"),
        P("mp", None),
        P("mp"),
        P("mp", ("groups", "seq")),
        P("mp", ("groups", "seq")),
        P(None, "mp"),
        P("groups"),
        P("groups"),
        P("groups"),
        P("groups"),
    )
    out_specs = (P("mp", ("groups", "seq")), P("mp", ("groups", "seq")))
    return jax.shard_map(body, mesh=mesh, in_specs=in_specs, out_specs=out_specs, check_vma=False)
```
